32 devices in a mesh: grp: 1, blk: 32 (over z, y, x, core), shot: 1.
Axes of the slice: x: 2, y: 2, z: 4, core: 2. Of those that a mesh axis runs over, the one named last changes fastest.
Arguments:
- adjoint_in: float32 [1, 2, 32, 8, 32, 256], P(('grp', 'shot'), None, 'blk'), may hold values from -6 to 6
- forward: float32 [1, 4, 32, 8, 32, 256], P(('grp', 'shot'), None, 'blk'), may hold values from -6 to 6
- modulus: float32 [32, 8, 32, 256], P(('grp', 'blk')), may hold values from 0.5 to 2
- buoyancy: float32 [32, 8, 32, 256], P(('grp', 'blk')), may hold values from 0.5 to 2
- topography: int32 [32, 8, 32], P(('grp', 'blk')), may hold values from 1 to 63
- receivers: int32 [4096, 2], P('grp'), may hold values from 0 to 127, as said below
- residuals: float32 [1, 2, 4096], P(('grp', 'shot')), may hold values from -6 to 6
Outputs:
- image_modulus: float32 [32, 8, 32, 256], P(('grp', 'blk'))
- image_buoyancy: float32 [32, 8, 32, 256], P(('grp', 'blk'))
- adjoint_out: float32 [1, 2, 32, 8, 32, 256], P(('grp', 'shot'), None, 'blk')
The draws below stay inside these ranges and needn't reach their ends.
Inputs may be any that keep to these rules, and one draw needn't show every extreme that they name: Column 0 holds indices below 64, column 1 indices below 128; several receivers may share a cell.
All inputs are finite; a program needn't handle non-finite values.
Results may differ from the reference program's by a relative error of at most 0.0003.
Values sent between devices are 32-bit elements; how exact they have to be, the bound alone decides.
No kernel may reach another device: no remote copies, remote signals or barrier semaphores. Data moves between devices by JAX's collectives and lax.ppermute only.
A program may use at most 64 MiB of HBM per device.

```python
import math
import jax
import jax.numpy as jnp

CX = 8
CY = 32
NZ = 256
NREC = 4096
STEPS = 2
YBLOCKS = 4
BLOCKS = 32
NX = 64
NY = 128
NSHOT = 1


def draw_receivers(key, part):
    key = jax.random.fold_in(key, 7)
    first, second = jax.random.split(key)
    across = jax.random.randint(first, (NREC,), 0, NX)
    along = jax.random.randint(second, (NREC,), 0, NY)
    across = across.at[0].set(NX - 1).at[1].set(0)
    along = along.at[0].set(0).at[1].set(NY - 1)
    return jnp.stack([across, along], axis=1).astype(jnp.int32)


def set_ends(result, key, least, high):
    shape = result.shape
    spot = [jax.random.randint(jax.random.fold_in(key, axis), (), 0, shape[axis]) for axis in range(len(shape))]
    result = result.at[tuple(spot)].set(least)
    longest = shape.index(max(shape))
    spot[longest] = (spot[longest] + 1) % shape[longest]
    return result.at[tuple(spot)].set(high)


def level_of(rng, shape, cuts, least, high):
    factor_of = 1.0
    for position, blocks in cuts:
        draws = jax.random.uniform(jax.random.fold_in(jax.random.fold_in(rng, 6), position), (blocks,), jnp.float32, least / len(cuts), high / len(cuts))
        factor_of = factor_of * jnp.repeat(jnp.exp(draws), shape[position] // blocks).reshape((-1,) + (1,) * (len(shape) - 1 - position))
    return factor_of


def centred(own_key, dims, spread, bound, cuts=(), kind=jnp.bfloat16):
    factor_of = level_of(own_key, dims, cuts, -0.22, 0.18) if cuts else 1.0
    result = jax.random.normal(own_key, dims, jnp.float32) * spread * factor_of
    return jnp.minimum(jnp.maximum(result, -bound), bound).astype(kind)


def setup_inputs(seed: int = 0, part: int = 0) -> dict:
    key_of = jax.random.split(jax.random.key(seed), 8)
    part_keys = jax.random.split(jax.random.fold_in(key_of[7], part), 8)
    adjoint_in = centred(part_keys[0], (NSHOT, 2, BLOCKS, CX, CY, NZ), 1.0, 6.0, ((2, 32),), jnp.float32)
    forward = centred(part_keys[1], (NSHOT, STEPS + 2, BLOCKS, CX, CY, NZ), 1.0, 6.0, ((2, 32),), jnp.float32)
    modulus = jnp.clip(jnp.exp(math.log(2.0) - 1.3862944 * jax.random.uniform(part_keys[2], (BLOCKS, CX, CY, NZ), jnp.float32) ** level_of(part_keys[2], (BLOCKS, CX, CY, NZ), ((0, 32),), -0.2, 0.2)), 0.5, 2.0)
    buoyancy = jnp.clip(jnp.exp(math.log(2.0) - 1.3862944 * jax.random.uniform(part_keys[3], (BLOCKS, CX, CY, NZ), jnp.float32) ** level_of(part_keys[3], (BLOCKS, CX, CY, NZ), ((0, 32),), -0.2, 0.2)), 0.5, 2.0)
    topography = set_ends(jax.random.randint(part_keys[4], (BLOCKS, CX, CY), 1, NZ // 4), jax.random.fold_in(part_keys[4], 1), 1, (NZ // 4) - 1).astype(jnp.int32)
    receivers = draw_receivers(jax.random.fold_in(jax.random.fold_in(key_of[7], part), 71), part)
    residuals = centred(part_keys[6], (NSHOT, STEPS, NREC), 1.0, 6.0, (), jnp.float32)
    return {"adjoint_in": adjoint_in, "forward": forward, "modulus": modulus, "buoyancy": buoyancy, "topography": topography, "receivers": receivers, "residuals": residuals}


laplace_coeffs = (-205.0 / 72.0, 8.0 / 5.0, -1.0 / 5.0, 8.0 / 315.0, -1.0 / 560.0)
slope_coeffs = (4.0 / 5.0, -1.0 / 5.0, 4.0 / 105.0, -1.0 / 280.0)
time_factor = 0.03


def window(padded, axis, offset, width_x, width_y, width_z):
    start = [4, 4, 4]
    start[axis] = start[axis] + offset
    return padded[start[0]:start[0] + width_x, start[1]:start[1] + width_y, start[2]:start[2] + width_z]


def stencil(extended, want_laplace):
    width_x = extended.shape[0] - 8
    width_y = extended.shape[1] - 8
    width_z = extended.shape[2]
    padded = jnp.pad(extended, ((0, 0), (0, 0), (4, 4)))
    centre = window(padded, 0, 0, width_x, width_y, width_z)
    laplace = 3.0 * laplace_coeffs[0] * centre
    slopes = []
    for axis in range(3):
        slope = jnp.zeros_like(centre)
        for offset in range(1, 5):
            upper = window(padded, axis, offset, width_x, width_y, width_z)
            lower = window(padded, axis, -offset, width_x, width_y, width_z)
            if want_laplace:
                laplace = laplace + laplace_coeffs[offset] * (upper + lower)
            slope = slope + slope_coeffs[offset - 1] * (upper - lower)
        slopes.append(slope)
    return laplace, slopes


def inject(receivers, topography, values, anchor_x, anchor_y, width_x, width_y, width_z):
    local_x = receivers[:, 0] - anchor_x
    local_y = receivers[:, 1] - anchor_y
    inside = (local_x >= 0) & (local_x < width_x) & (local_y >= 0) & (local_y < width_y)
    safe_x = jnp.clip(local_x, 0, width_x - 1)
    safe_y = jnp.clip(local_y, 0, width_y - 1)
    column = topography[safe_x, safe_y] + 1
    flat = jnp.where(inside, (safe_x * width_y + safe_y) * width_z + column, width_x * width_y * width_z)
    placed = jnp.zeros((width_x * width_y * width_z,), jnp.float32).at[flat].add(values, mode="drop")
    return placed.reshape(width_x, width_y, width_z)


def assemble(blocked):
    rest = blocked.shape[3:]
    rows = blocked.shape[0] // YBLOCKS
    grid = blocked.reshape((rows, YBLOCKS) + blocked.shape[1:])
    grid = jnp.moveaxis(grid, 2, 1)
    return grid.reshape((rows * blocked.shape[1], YBLOCKS * blocked.shape[2]) + rest)


def split_blocks(grid, width_x, width_y):
    rest = grid.shape[2:]
    rows = grid.shape[0] // width_x
    parted = grid.reshape((rows, width_x, YBLOCKS, width_y) + rest)
    parted = jnp.moveaxis(parted, 2, 1)
    return parted.reshape((rows * YBLOCKS, width_x, width_y) + rest)


def pad_plane(field):
    return jnp.pad(field, ((4, 4), (4, 4), (0, 0)))


def reference(adjoint_in, forward, modulus, buoyancy, topography, receivers, residuals):
    block_x, block_y = modulus.shape[1], modulus.shape[2]
    modulus_grid = assemble(modulus)
    buoyancy_grid = assemble(buoyancy)
    topo_grid = assemble(topography)
    width_x, width_y, width_z = modulus_grid.shape
    depth = jax.lax.broadcasted_iota(jnp.int32, (width_x, width_y, width_z), 2)
    mask = (depth >= topo_grid[:, :, None]).astype(jnp.float32)
    grad_buoy = stencil(pad_plane(buoyancy_grid), False)[1]
    image_mod = jnp.zeros((width_x, width_y, width_z), jnp.float32)
    image_buo = jnp.zeros((width_x, width_y, width_z), jnp.float32)
    states = []
    for shot_index in range(NSHOT):
        later = assemble(adjoint_in[shot_index, 0])
        current = assemble(adjoint_in[shot_index, 1])
        fields = [assemble(forward[shot_index, level]) for level in range(STEPS + 2)]
        shot_states = []
        for level in range(STEPS):
            scaled = mask * modulus_grid * current
            laplace, slopes = stencil(pad_plane(scaled), True)
            operated = buoyancy_grid * laplace
            for axis in range(3):
                operated = operated + grad_buoy[axis] * slopes[axis]
            source = inject(receivers, topo_grid, residuals[shot_index, level], 0, 0, width_x, width_y, width_z)
            earlier = mask * (2.0 * current - later + time_factor * operated + source)
            image_mod = image_mod + current * (fields[level] - 2.0 * fields[level + 1] + fields[level + 2])
            forward_slopes = stencil(pad_plane(fields[level + 1]), False)[1]
            for axis in range(3):
                image_buo = image_buo + forward_slopes[axis] * slopes[axis]
            shot_states.append(split_blocks(earlier, block_x, block_y))
            later = current
            current = earlier
        states.append(jnp.stack(shot_states))
    return split_blocks(image_mod, block_x, block_y), split_blocks(image_buo, block_x, block_y), jnp.stack(states)
```

```python
import jax
import jax.numpy as jnp
from jax import lax
from jax.sharding import PartitionSpec as P

STEPS = 2
YBLOCKS = 4


laplace_coeffs = (-205.0 / 72.0, 8.0 / 5.0, -1.0 / 5.0, 8.0 / 315.0, -1.0 / 560.0)
slope_coeffs = (4.0 / 5.0, -1.0 / 5.0, 4.0 / 105.0, -1.0 / 280.0)
time_factor = 0.03


def shifted(value, axis, by):
    size = lax.axis_size(axis)
    pairs = [(i, i + by) for i in range(size) if 0 <= i + by < size]
    return lax.ppermute(value, axis, pairs)


def window(padded, axis, offset, width_x, width_y, width_z):
    start = [4, 4, 4]
    start[axis] = start[axis] + offset
    return padded[
        start[0] : start[0] + width_x, start[1] : start[1] + width_y, start[2] : start[2] + width_z
    ]


def stencil(extended, want_laplace):
    width_x = extended.shape[0] - 8
    width_y = extended.shape[1] - 8
    width_z = extended.shape[2]
    padded = jnp.pad(extended, ((0, 0), (0, 0), (4, 4)))
    centre = window(padded, 0, 0, width_x, width_y, width_z)
    laplace = 3.0 * laplace_coeffs[0] * centre
    slopes = []
    for axis in range(3):
        slope = jnp.zeros_like(centre)
        for offset in range(1, 5):
            upper = window(padded, axis, offset, width_x, width_y, width_z)
            lower = window(padded, axis, -offset, width_x, width_y, width_z)
            if want_laplace:
                laplace = laplace + laplace_coeffs[offset] * (upper + lower)
            slope = slope + slope_coeffs[offset - 1] * (upper - lower)
        slopes.append(slope)
    return (laplace, slopes)


def inject(receivers, topography, values, anchor_x, anchor_y, width_x, width_y, width_z):
    in_x = receivers[:, 0][None, :] - anchor_x == lax.broadcasted_iota(jnp.int32, (width_x, 1), 0)
    in_y = receivers[:, 1][None, :] - anchor_y == lax.broadcasted_iota(jnp.int32, (width_y, 1), 0)
    plane = lax.dot_general(
        jnp.where(in_x, values[None, :], 0.0),
        in_y.astype(jnp.float32),
        (((1,), (1,)), ((), ())),
        precision=lax.Precision.HIGHEST,
    )
    depth = lax.broadcasted_iota(jnp.int32, (width_x, width_y, width_z), 2)
    return jnp.where(depth == topography[:, :, None] + 1, plane[:, :, None], 0.0)


def extend(stack):
    column_index = lax.axis_index("blk") % YBLOCKS
    below_x = shifted(stack[:, -4:], "blk", YBLOCKS)
    above_x = shifted(stack[:, :4], "blk", -YBLOCKS)
    below_y = shifted(stack[:, :, -4:], "blk", 1)
    above_y = shifted(stack[:, :, :4], "blk", -1)
    below_y = jnp.where(column_index > 0, below_y, 0.0)
    above_y = jnp.where(column_index < YBLOCKS - 1, above_y, 0.0)
    middle = jnp.concatenate([below_y, stack, above_y], axis=2)
    edge = ((0, 0), (0, 0), (4, 4), (0, 0))
    return jnp.concatenate([jnp.pad(below_x, edge), middle, jnp.pad(above_x, edge)], axis=1)


def shards(adjoint_in, forward, modulus, buoyancy, topography, receivers, residuals):
    modulus = modulus[0]
    buoyancy = buoyancy[0]
    topography = topography[0]
    width_x, width_y, width_z = modulus.shape
    index = lax.axis_index("blk")
    anchor_x = index // YBLOCKS * width_x
    anchor_y = index % YBLOCKS * width_y
    depth = lax.broadcasted_iota(jnp.int32, (width_x, width_y, width_z), 2)
    mask = (depth >= topography[:, :, None]).astype(jnp.float32)
    fields = forward[0, :, 0]
    later = adjoint_in[0, 0, 0]
    current = adjoint_in[0, 1, 0]
    image_mod = jnp.zeros((width_x, width_y, width_z), jnp.float32)
    image_buo = jnp.zeros((width_x, width_y, width_z), jnp.float32)
    statics = jnp.concatenate([buoyancy[None], fields[1 : STEPS + 1]], axis=0)
    fixed = extend(statics)
    grad_buoy = stencil(fixed[0], False)[1]
    states = []
    for level in range(STEPS):
        scaled = mask * modulus * current
        adjoint_ext = extend(scaled[None])[0]
        forward_ext = fixed[level + 1]
        laplace, slopes = stencil(adjoint_ext, True)
        operated = buoyancy * laplace
        for axis in range(3):
            operated = operated + grad_buoy[axis] * slopes[axis]
        source = inject(
            receivers,
            topography,
            residuals[0, level],
            anchor_x,
            anchor_y,
            width_x,
            width_y,
            width_z,
        )
        earlier = mask * (2.0 * current - later + time_factor * operated + source)
        term_mod = current * (fields[level] - 2.0 * fields[level + 1] + fields[level + 2])
        forward_slopes = stencil(forward_ext, False)[1]
        term_buo = (
            forward_slopes[0] * slopes[0]
            + forward_slopes[1] * slopes[1]
            + forward_slopes[2] * slopes[2]
        )
        image_mod = image_mod + term_mod
        image_buo = image_buo + term_buo
        states.append(earlier)
        later = current
        current = earlier
    totals = lax.psum(jnp.stack([image_mod, image_buo]), "shot")
    image_mod = totals[0]
    image_buo = totals[1]
    return (image_mod[None], image_buo[None], jnp.stack(states)[None, :, None])


def solution(mesh):
    placed = (
        P(("grp", "shot"), None, "blk", None, None, None),
        P(("grp", "shot"), None, "blk", None, None, None),
        P(("grp", "blk"), None, None, None),
        P(("grp", "blk"), None, None, None),
        P(("grp", "blk"), None, None),
        P("grp", None),
        P(("grp", "shot"), None, None),
    )
    return jax.shard_map(
        shards,
        mesh=mesh,
        in_specs=placed,
        out_specs=(
            P(("grp", "blk"), None, None, None),
            P(("grp", "blk"), None, None, None),
            P(("grp", "shot"), None, "blk", None, None, None),
        ),
        check_vma=False,
    )
```

```python
import numpy as np
import jax
import jax.numpy as jnp
from jax import lax
from jax.experimental import pallas as pl
from jax.experimental.pallas import tpu as pltpu
from jax.sharding import PartitionSpec as P

STEPS = 2
YBLOCKS = 4
HALO = 4

A0 = -205.0 / 72.0
A = (8.0 / 5.0, -1.0 / 5.0, 8.0 / 315.0, -1.0 / 560.0)
C = (4.0 / 5.0, -1.0 / 5.0, 4.0 / 105.0, -1.0 / 280.0)
A_INT = (8064.0, -1008.0, 128.0, -9.0)
C_INT = (672.0, -168.0, 32.0, -3.0)
A_UNIT = 1.0 / 5040.0
C_UNIT = 1.0 / 840.0
TIME = 0.03
F32 = jnp.float32
BF16 = jnp.bfloat16
VMEM = pltpu.VMEM


def row_pairs(size):
    first, second = [], []
    for i in range(size):
        r = i // YBLOCKS
        partner = i + YBLOCKS if r % 2 == 0 else i - YBLOCKS
        if 0 <= partner < size:
            first.append((i, partner))
        partner = i + YBLOCKS if r % 2 == 1 else i - YBLOCKS
        if 0 <= partner < size:
            second.append((i, partner))
    return first, second


def column_pairs(size):
    first, second = [], []
    for i in range(size):
        c = i % YBLOCKS
        partner = c + 1 if c % 2 == 0 else c - 1
        if 0 <= partner < YBLOCKS:
            first.append((i, i - c + partner))
        partner = c + 1 if c % 2 == 1 else c - 1
        if 0 <= partner < YBLOCKS:
            second.append((i, i - c + partner))
    return first, second


def along_z(depth):
    lap = np.zeros((depth, depth), np.float32)
    slope = np.zeros((depth, depth), np.float32)
    for k in range(1, HALO + 1):
        i = np.arange(depth - k)
        lap[i + k, i] += A_INT[k - 1]
        lap[i, i + k] += A_INT[k - 1]
        slope[i + k, i] += C_INT[k - 1]
        slope[i, i + k] -= C_INT[k - 1]
    return np.concatenate([slope, lap], axis=1)


def along_y(height):
    out = []
    for parity in range(2):
        full = np.zeros((2, height, height + 2 * HALO), np.float32)
        for i in range(height):
            for k in range(1, HALO + 1):
                full[0, i, HALO + i + k] += C_INT[k - 1]
                full[0, i, HALO + i - k] -= C_INT[k - 1]
                full[1, i, HALO + i + k] += A_INT[k - 1]
                full[1, i, HALO + i - k] += A_INT[k - 1]
        full = full.reshape(2 * height, height + 2 * HALO)
        low, own, high = full[:, :HALO], full[:, HALO:-HALO], full[:, -HALO:]
        edge = np.concatenate([high, low] if parity == 0 else [low, high], axis=1)
        out.append(np.concatenate([own, own, edge, edge], axis=1))
    return np.stack(out)


def parts(value):
    lead = value.astype(BF16)
    return lead, (value - lead.astype(F32)).astype(BF16)


def dot(a, b):
    return jnp.dot(a, b, preferred_element_type=F32)


def z_product(block, factor):
    planes, height, depth = block.shape
    lead, trail = parts(block.reshape(planes * height, depth))
    out = dot(lead, factor) + dot(trail, factor)
    return out.reshape(planes, height, out.shape[1])


def y_product(plane, first, second, factor):
    lead, trail = parts(plane)
    edge = jnp.concatenate([first, second], axis=0)
    edge_lead = edge.astype(BF16).astype(F32)
    edges = jnp.concatenate([edge_lead, edge - edge_lead], axis=0).astype(BF16)
    return dot(factor, jnp.concatenate([lead, trail, edges], axis=0))


def x_slope(own):
    out = []
    for i in range(len(own)):
        total = None
        for k in range(1, HALO + 1):
            if i + k < len(own) and i - k >= 0:
                term = C[k - 1] * (own[i + k] - own[i - k])
            elif i + k < len(own):
                term = C[k - 1] * own[i + k]
            elif i - k >= 0:
                term = -C[k - 1] * own[i - k]
            else:
                continue
            total = term if total is None else total + term
        out.append(total)
    return out


def x_laplace(own):
    out = []
    for i in range(len(own)):
        total = 3.0 * A0 * own[i]
        for k in range(1, HALO + 1):
            if i + k < len(own) and i - k >= 0:
                total = total + A[k - 1] * (own[i + k] + own[i - k])
            elif i + k < len(own):
                total = total + A[k - 1] * own[i + k]
            elif i - k >= 0:
                total = total + A[k - 1] * own[i - k]
        out.append(total)
    return out


def edge_terms(i, count, low, high):
    terms = []
    for k in range(1, HALO + 1):
        if i - k < 0:
            terms.append((k, -1.0, low[HALO + i - k]))
        if i + k >= count:
            terms.append((k, 1.0, high[i + k - count]))
    return terms


def edge_slope(i, count, low, high):
    total = None
    for k, sign, value in edge_terms(i, count, low, high):
        term = (sign * C[k - 1]) * value
        total = term if total is None else total + term
    return total


def edge_laplace(i, count, low, high):
    total = None
    for k, _, value in edge_terms(i, count, low, high):
        term = A[k - 1] * value
        total = term if total is None else total + term
    return total


def depth_of_surface(topo_row, height):
    rows = lax.broadcasted_iota(jnp.int32, (height, height), 0)
    lanes = lax.broadcasted_iota(jnp.int32, (height, height), 1)
    picked = jnp.where(rows == lanes, topo_row.astype(F32), 0.0)
    return jnp.sum(picked, axis=1, keepdims=True).astype(jnp.int32)


def row_parity():
    return lax.rem(lax.axis_index("blk") // YBLOCKS, 2)


def column_parity():
    return lax.rem(lax.rem(lax.axis_index("blk"), YBLOCKS), 2)


def copy_all(pairs, sem):
    copies = [pltpu.make_async_copy(a, b, sem.at[n]) for n, (a, b) in enumerate(pairs)]
    for c in copies:
        c.start()
    return copies


def first_kernel(adj, mod, buoy, topo, x1, x2, s0, cur_v, mod_v, sem):
    width, height, depth = s0.shape
    parity = row_parity()
    high_first = (1 - parity) * HALO
    low_first = parity * HALO
    copies = copy_all(
        [
            (adj.at[0, 1, 0], cur_v),
            (mod.at[0], mod_v),
            (buoy.at[0, pl.ds(high_first, HALO)], x1.at[0]),
            (buoy.at[0, pl.ds(low_first, HALO)], x2.at[0]),
        ],
        sem,
    )
    lanes = lax.broadcasted_iota(jnp.int32, (height, depth), 1)
    masks = [lanes >= depth_of_surface(topo[0, i : i + 1, :], height) for i in range(width)]
    copies[0].wait()
    copies[1].wait()
    for i in range(width):
        s0[i] = jnp.where(masks[i], mod_v[i] * cur_v[i], 0.0)
    x1[1] = s0[pl.ds(high_first, HALO)]
    x2[1] = s0[pl.ds(low_first, HALO)]
    copies[2].wait()
    copies[3].wait()


def second_kernel(buoy, fwd, s0, x1, x2, y1, y2, buoy_v, fields_v, sem):
    width, height, depth = s0.shape
    parity = row_parity()
    high_first = (1 - parity) * HALO
    low_first = parity * HALO
    copies = copy_all(
        [
            (buoy.at[0], buoy_v),
            (fwd.at[0, pl.ds(1, 2), 0], fields_v),
            (fwd.at[0, pl.ds(1, 2), 0, pl.ds(high_first, HALO)], x1),
            (fwd.at[0, pl.ds(1, 2), 0, pl.ds(low_first, HALO)], x2),
        ],
        sem,
    )
    even = column_parity() == 0

    def pack(n, value):
        low = value[:, :HALO]
        high = value[:, height - HALO :]
        y1[n] = jnp.where(even, high, low)
        y2[n] = jnp.where(even, low, high)

    pack(1, s0[...])
    copies[0].wait()
    pack(0, buoy_v[...])
    copies[1].wait()
    pack(2, fields_v[0])
    pack(3, fields_v[1])
    copies[2].wait()
    copies[3].wait()


def early_kernel(
    cur, later, mod, buoy, topo, s0, rec, res, y1, y2, zf, yf,
    rest, sx_own, sy, sz, gx_own, gy, gz, weight, scale, source,
    zs, zb, ys, yb,
):
    width, height, depth = s0.shape
    size = lax.axis_index("blk")
    anchor_x = size // YBLOCKS * width
    anchor_y = lax.rem(size, YBLOCKS) * height
    factor_y = yf[column_parity()]
    count = rec.shape[1]
    rx = rec[0:1, :] - anchor_x
    ry = rec[1:2, :] - anchor_y
    ids = lax.broadcasted_iota(jnp.int32, (STEPS * width, count), 0)
    values = jnp.concatenate(
        [jnp.broadcast_to(res[0, s : s + 1, :], (width, count)) for s in range(STEPS)], axis=0
    )
    hit_x = jnp.where(lax.rem(ids, width) == rx, values, 0.0)
    hit_y = (lax.broadcasted_iota(jnp.int32, (height, count), 0) == ry).astype(F32)
    plane = lax.dot_general(
        hit_y,
        hit_x,
        (((1,), (1,)), ((), ())),
        precision=lax.Precision.HIGHEST,
        preferred_element_type=F32,
    )
    zs[...] = z_product(s0[...], zf[...])
    zb[...] = z_product(buoy[0], zf[:, :depth])
    for i in range(width):
        ys[i] = y_product(s0[i], y1[1, i], y2[1, i], factor_y)
        yb[i] = y_product(buoy[0, i], y1[0, i], y2[0, i], factor_y[:height])
    lanes = lax.broadcasted_iota(jnp.int32, (height, depth), 1)
    for i in range(width):
        surface = depth_of_surface(topo[0, i : i + 1, :], height)
        live = lanes >= surface
        at = lanes == surface + 1
        scale[i] = jnp.where(live, TIME, 0.0)
        for s in range(STEPS):
            n = s * width + i
            source[s, i] = jnp.where(at, plane[:, n : n + 1], 0.0)
    for t in range(height // 8):
        rows = pl.ds(8 * t, 8)
        own = [s0[i, rows] for i in range(width)]
        slope = x_slope(own)
        laplace = x_laplace(own)
        for i in range(width):
            sx_own[i, rows] = slope[i]
            edge = ys[i, pl.ds(height + 8 * t, 8)] + zs[i, rows, depth:]
            laplace[i] = laplace[i] + A_UNIT * edge
        own = [buoy[0, i, rows] for i in range(width)]
        slope = x_slope(own)
        for i in range(width):
            w = scale[i, rows]
            gx_own[i, rows] = slope[i] * w
            g_y = (C_UNIT * w) * yb[i, rows]
            g_z = (C_UNIT * w) * zb[i, rows]
            s_y = C_UNIT * ys[i, rows]
            s_z = C_UNIT * zs[i, rows, :depth]
            b = own[i] * w
            weight[i, rows] = b
            gy[i, rows] = g_y
            gz[i, rows] = g_z
            sy[i, rows] = s_y
            sz[i, rows] = s_z
            moved = 2.0 * cur[0, 0, 0, i, rows] - later[0, 0, 0, i, rows] + source[0, i, rows]
            moved = jnp.where(w > 0.0, moved, 0.0)
            rest[i, rows] = moved + b * laplace[i] + g_y * s_y + g_z * s_z


def finish_kernel(
    xa1, xa2, rest, sx_own, gx_own, weight, scale, mod,
    e0, s1, sx, gx, x1, x2, y1, y2,
):
    width, height, depth = e0.shape

    def body(low_ref, high_ref, low_out, high_out):
        for t in range(height // 8):
            rows = pl.ds(8 * t, 8)
            low = [low_ref[1, i, rows] for i in range(HALO)]
            high = [high_ref[1, i, rows] for i in range(HALO)]
            low_b = [low_ref[0, i, rows] for i in range(HALO)]
            high_b = [high_ref[0, i, rows] for i in range(HALO)]
            for i in range(width):
                s_x = sx_own[i, rows] + edge_slope(i, width, low, high)
                g_x = gx_own[i, rows] + scale[i, rows] * edge_slope(i, width, low_b, high_b)
                earlier = (
                    rest[i, rows]
                    + weight[i, rows] * edge_laplace(i, width, low, high)
                    + g_x * s_x
                )
                scaled = mod[0, i, rows] * earlier
                sx[i, rows] = s_x
                gx[i, rows] = g_x
                e0[i, rows] = earlier
                s1[i, rows] = scaled
                if i < HALO:
                    low_out[i, rows] = scaled
                if i >= width - HALO:
                    high_out[i - (width - HALO), rows] = scaled

    @pl.when(row_parity() == 0)
    def _():
        body(xa2, xa1, x2, x1)

    @pl.when(row_parity() == 1)
    def _():
        body(xa1, xa2, x1, x2)

    even = column_parity() == 0
    low = s1[:, :HALO]
    high = s1[:, height - HALO :]
    y1[...] = jnp.where(even, high, low)
    y2[...] = jnp.where(even, low, high)


def middle_kernel(
    cur, e0, s1, sx0, sy0, sz0, gy, gz, weight, scale, source, fwd, xf1, xf2, yf1, yf2, y1, y2, zf, yf,
    rest, sx_own, image, fx, image_mod,
    zs, ys, z1, z2, ya, yb,
):
    width, height, depth = e0.shape
    factor_y = yf[column_parity()]
    zs[...] = z_product(s1[...], zf[...])
    z1[...] = z_product(fwd[0, 1, 0], zf[:, :depth])
    z2[...] = z_product(fwd[0, 2, 0], zf[:, :depth])
    for i in range(width):
        ys[i] = y_product(s1[i], y1[i], y2[i], factor_y)
        ya[i] = y_product(fwd[0, 1, 0, i], yf1[2, i], yf2[2, i], factor_y[:height])
        yb[i] = y_product(fwd[0, 2, 0, i], yf1[3, i], yf2[3, i], factor_y[:height])

    def body(low_ref, high_ref):
        for t in range(height // 8):
            rows = pl.ds(8 * t, 8)
            own = [s1[i, rows] for i in range(width)]
            slope = x_slope(own)
            laplace = x_laplace(own)
            own1 = [fwd[0, 1, 0, i, rows] for i in range(width)]
            own2 = [fwd[0, 2, 0, i, rows] for i in range(width)]
            slope1 = x_slope(own1)
            slope2 = x_slope(own2)
            low1 = [low_ref[0, i, rows] for i in range(HALO)]
            high1 = [high_ref[0, i, rows] for i in range(HALO)]
            low2 = [low_ref[1, i, rows] for i in range(HALO)]
            high2 = [high_ref[1, i, rows] for i in range(HALO)]
            for i in range(width):
                now, before = cur[0, 0, 0, i, rows], e0[i, rows]
                s_y = C_UNIT * ys[i, rows]
                s_z = C_UNIT * zs[i, rows, :depth]
                edge = ys[i, pl.ds(height + 8 * t, 8)] + zs[i, rows, depth:]
                lap = laplace[i] + A_UNIT * edge
                moved = 2.0 * before - now + source[1, i, rows]
                moved = jnp.where(scale[i, rows] > 0.0, moved, 0.0)
                rest[i, rows] = (
                    moved + weight[i, rows] * lap + gy[i, rows] * s_y + gz[i, rows] * s_z
                )
                sx_own[i, rows] = slope[i]
                f1x = slope1[i] + edge_slope(i, width, low1, high1)
                fx[i, rows] = slope2[i] + edge_slope(i, width, low2, high2)
                image[i, rows] = (
                    f1x * sx0[i, rows]
                    + C_UNIT
                    * (
                        ya[i, rows] * sy0[i, rows]
                        + z1[i, rows] * sz0[i, rows]
                        + yb[i, rows] * s_y
                        + z2[i, rows] * s_z
                    )
                )
                f0, f3 = fwd[0, 0, 0, i, rows], fwd[0, 3, 0, i, rows]
                image_mod[0, i, rows] = now * (f0 - 2.0 * own1[i] + own2[i]) + before * (
                    own1[i] - 2.0 * own2[i] + f3
                )

    @pl.when(row_parity() == 0)
    def _():
        body(xf2, xf1)

    @pl.when(row_parity() == 1)
    def _():
        body(xf1, xf2)


def last_kernel(
    xs1, xs2, rest, sx_own, image, fx, gx, weight, e0,
    image_out, states_out,
    image_v, e1_v, sem,
):
    width, height, depth = e0.shape
    first = pltpu.make_async_copy(e0, states_out.at[0, 0, 0], sem.at[0])
    first.start()

    def body(low_ref, high_ref):
        for t in range(height // 8):
            rows = pl.ds(8 * t, 8)
            low = [low_ref[i, rows] for i in range(HALO)]
            high = [high_ref[i, rows] for i in range(HALO)]
            for i in range(width):
                s_x = sx_own[i, rows] + edge_slope(i, width, low, high)
                e1_v[i, rows] = (
                    rest[i, rows]
                    + weight[i, rows] * edge_laplace(i, width, low, high)
                    + gx[i, rows] * s_x
                )
                image_v[i, rows] = image[i, rows] + fx[i, rows] * s_x

    @pl.when(row_parity() == 0)
    def _():
        body(xs2, xs1)

    @pl.when(row_parity() == 1)
    def _():
        body(xs1, xs2)

    second = pltpu.make_async_copy(e1_v, states_out.at[0, 1, 0], sem.at[1])
    third = pltpu.make_async_copy(image_v, image_out.at[0], sem.at[2])
    second.start()
    third.start()
    first.wait()
    second.wait()
    third.wait()


def call(kernel, name, inputs, outputs, scratch=(), us=1.0):
    arrays, in_specs = [], []
    for array, near in inputs:
        if near:
            array = pltpu.with_memory_space_constraint(array, VMEM)
        arrays.append(array)
        in_specs.append(pl.BlockSpec(memory_space=VMEM if near else pl.ANY))
    shapes, out_specs = [], []
    for shape, near in outputs:
        shapes.append(VMEM(shape, F32) if near else jax.ShapeDtypeStruct(shape, F32))
        out_specs.append(pl.BlockSpec(memory_space=VMEM if near else pl.ANY))
    return pl.pallas_call(
        kernel,
        name=name,
        in_specs=in_specs,
        out_specs=out_specs,
        out_shape=shapes,
        scratch_shapes=list(scratch),
        compiler_params=pltpu.CompilerParams(vmem_limit_bytes=16 * 1024 * 1024),
        cost_estimate=pl.CostEstimate(
            flops=0, bytes_accessed=int(us * 3.0e6), transcendentals=0
        ),
    )(*arrays)


def shards(adjoint_in, forward, modulus, buoyancy, topography, receivers, residuals):
    width, height, depth = modulus.shape[1:]
    block = (width, height, depth)
    size = lax.axis_size("blk")
    rows1, rows2 = row_pairs(size)
    cols1, cols2 = column_pairs(size)
    zf = jnp.asarray(along_z(depth), BF16)
    yf = jnp.asarray(along_y(height), BF16)
    dma = pltpu.SemaphoreType.DMA

    def swap(value, pairs):
        return lax.ppermute(value, "blk", pairs)

    ahead = (2, HALO, height, depth)
    xa1, xa2, s0 = call(
        first_kernel,
        "scaled_and_planes",
        [(adjoint_in, False), (modulus, False), (buoyancy, False), (topography, True)],
        [(ahead, True), (ahead, True), (block, True)],
        [VMEM(block, F32), VMEM(block, F32), dma((4,))],
    )
    xa1, xa2 = swap(xa1, rows1), swap(xa2, rows2)
    edge = (4, width, HALO, depth)
    xf1, xf2, ya1, ya2 = call(
        second_kernel,
        "edges",
        [(buoyancy, False), (forward, False), (s0, True)],
        [(ahead, True), (ahead, True), (edge, True), (edge, True)],
        [VMEM(block, F32), VMEM((2,) + block, F32), dma((4,))],
    )
    ya1, ya2 = swap(ya1, cols1), swap(ya2, cols2)
    xf1, xf2 = swap(xf1, rows1), swap(xf2, rows2)
    later = adjoint_in[:, :1]
    current = adjoint_in[:, 1:]
    z_out = (width, height, 2 * depth)
    y_out = (width, 2 * height, depth)
    rest, sx_own, sy, sz, gx_own, gy, gz, weight, scale, source = call(
        early_kernel,
        "step0_own",
        [(current, True), (later, True), (modulus, True), (buoyancy, True), (topography, True), (s0, True),
         (receivers.T, True), (residuals, True), (ya1, True), (ya2, True), (zf, True), (yf, True)],
        [(block, True)] * 9 + [((STEPS,) + block, True)],
        [VMEM(z_out, F32), VMEM(block, F32), VMEM(y_out, F32), VMEM(block, F32)],
        us=4.0,
    )
    half = (HALO, height, depth)
    side = (width, HALO, depth)
    e0, s1, sx, gx, xs1, xs2, ys1, ys2 = call(
        finish_kernel,
        "step0_planes",
        [(xa1, True), (xa2, True), (rest, True), (sx_own, True), (gx_own, True), (weight, True), (scale, True),
         (modulus, True)],
        [(block, True)] * 4 + [(half, True)] * 2 + [(side, True)] * 2,
    )
    xs1, xs2 = swap(xs1, rows1), swap(xs2, rows2)
    ys1, ys2 = swap(ys1, cols1), swap(ys2, cols2)
    rest, sx_own, image, fx, image_mod = call(
        middle_kernel,
        "images_and_step1_own",
        [(current, True), (e0, True), (s1, True), (sx, True), (sy, True), (sz, True), (gy, True), (gz, True),
         (weight, True), (scale, True), (source, True), (forward, True), (xf1, True), (xf2, True), (ya1, True),
         (ya2, True), (ys1, True), (ys2, True), (zf, True), (yf, True)],
        [(block, True)] * 4 + [((1,) + block, True)],
        [VMEM(z_out, F32), VMEM(y_out, F32)] + [VMEM(block, F32)] * 4,
        us=5.0,
    )
    image_buo, states = call(
        last_kernel,
        "step1_planes",
        [(xs1, True), (xs2, True), (rest, True), (sx_own, True), (image, True), (fx, True), (gx, True),
         (weight, True), (e0, True)],
        [((1,) + block, False), ((1, STEPS, 1) + block, False)],
        [VMEM(block, F32), VMEM(block, F32), dma((3,))],
    )
    if lax.axis_size("shot") > 1:
        image_mod, image_buo = lax.psum((image_mod, image_buo), "shot")
    return image_mod, image_buo, states


def solution(mesh):
    placed = (
        P(("grp", "shot"), None, "blk", None, None, None),
        P(("grp", "shot"), None, "blk", None, None, None),
        P(("grp", "blk"), None, None, None),
        P(("grp", "blk"), None, None, None),
        P(("grp", "blk"), None, None),
        P("grp", None),
        P(("grp", "shot"), None, None),
    )
    return jax.shard_map(
        shards,
        mesh=mesh,
        in_specs=placed,
        out_specs=(
            P(("grp", "blk"), None, None, None),
            P(("grp", "blk"), None, None, None),
            P(("grp", "shot"), None, "blk", None, None, None),
        ),
        check_vma=False,
    )
```

```python
import numpy as np
import jax
import jax.numpy as jnp
from jax import lax
from jax.experimental import pallas as pl
from jax.experimental.pallas import tpu as pltpu
from jax.sharding import PartitionSpec as P

STEPS = 2
YBLOCKS = 4
HALO = 4

A0 = -205.0 / 72.0
A = (8.0 / 5.0, -1.0 / 5.0, 8.0 / 315.0, -1.0 / 560.0)
C = (4.0 / 5.0, -1.0 / 5.0, 4.0 / 105.0, -1.0 / 280.0)
A_INT = (8064.0, -1008.0, 128.0, -9.0)
C_INT = (672.0, -168.0, 32.0, -3.0)
A_UNIT = 1.0 / 5040.0
C_UNIT = 1.0 / 840.0
TIME = 0.03
F32 = jnp.float32
BF16 = jnp.bfloat16
VMEM = pltpu.VMEM


def row_pairs(size):
    first, second = [], []
    for i in range(size):
        r = i // YBLOCKS
        partner = i + YBLOCKS if r % 2 == 0 else i - YBLOCKS
        if 0 <= partner < size:
            first.append((i, partner))
        partner = i + YBLOCKS if r % 2 == 1 else i - YBLOCKS
        if 0 <= partner < size:
            second.append((i, partner))
    return first, second


def column_pairs(size):
    first, second = [], []
    for i in range(size):
        c = i % YBLOCKS
        partner = c + 1 if c % 2 == 0 else c - 1
        if 0 <= partner < YBLOCKS:
            first.append((i, i - c + partner))
        partner = c + 1 if c % 2 == 1 else c - 1
        if 0 <= partner < YBLOCKS:
            second.append((i, i - c + partner))
    return first, second


def along_z(depth):
    lap = np.zeros((depth, depth), np.float32)
    slope = np.zeros((depth, depth), np.float32)
    for k in range(1, HALO + 1):
        i = np.arange(depth - k)
        lap[i + k, i] += A_INT[k - 1]
        lap[i, i + k] += A_INT[k - 1]
        slope[i + k, i] += C_INT[k - 1]
        slope[i, i + k] -= C_INT[k - 1]
    return np.concatenate([slope, lap], axis=1)


def along_y(height):
    out = []
    for parity in range(2):
        full = np.zeros((2, height, height + 2 * HALO), np.float32)
        for i in range(height):
            for k in range(1, HALO + 1):
                full[0, i, HALO + i + k] += C_INT[k - 1]
                full[0, i, HALO + i - k] -= C_INT[k - 1]
                full[1, i, HALO + i + k] += A_INT[k - 1]
                full[1, i, HALO + i - k] += A_INT[k - 1]
        full = full.reshape(2 * height, height + 2 * HALO)
        low, own, high = full[:, :HALO], full[:, HALO:-HALO], full[:, -HALO:]
        edge = np.concatenate([high, low] if parity == 0 else [low, high], axis=1)
        out.append(np.concatenate([own, own, edge, edge], axis=1))
    return np.stack(out)


def edge_rows(factor, height):
    rows = np.concatenate([np.arange(8), np.arange(height - 8, height)])
    return factor[:, np.concatenate([rows, height + rows]), 2 * height :]


def parts(value):
    lead = value.astype(BF16)
    return lead, (value - lead.astype(F32)).astype(BF16)


def dot(a, b):
    return jnp.dot(a, b, preferred_element_type=F32)


def z_product(block, factor):
    planes, height, depth = block.shape
    lead, trail = parts(block.reshape(planes * height, depth))
    out = dot(lead, factor) + dot(trail, factor)
    return out.reshape(planes, height, out.shape[1])


def edge_parts(first, second):
    edge = jnp.concatenate([first, second], axis=0)
    lead = edge.astype(BF16).astype(F32)
    return jnp.concatenate([lead, edge - lead], axis=0).astype(BF16)


def y_product(plane, first, second, factor):
    lead, trail = parts(plane)
    return dot(factor, jnp.concatenate([lead, trail, edge_parts(first, second)], axis=0))


def x_slope(own):
    out = []
    for i in range(len(own)):
        total = None
        for k in range(1, HALO + 1):
            if i + k < len(own) and i - k >= 0:
                term = C[k - 1] * (own[i + k] - own[i - k])
            elif i + k < len(own):
                term = C[k - 1] * own[i + k]
            elif i - k >= 0:
                term = -C[k - 1] * own[i - k]
            else:
                continue
            total = term if total is None else total + term
        out.append(total)
    return out


def x_laplace(own):
    out = []
    for i in range(len(own)):
        total = 3.0 * A0 * own[i]
        for k in range(1, HALO + 1):
            if i + k < len(own) and i - k >= 0:
                total = total + A[k - 1] * (own[i + k] + own[i - k])
            elif i + k < len(own):
                total = total + A[k - 1] * own[i + k]
            elif i - k >= 0:
                total = total + A[k - 1] * own[i - k]
        out.append(total)
    return out


def edge_terms(i, count, low, high):
    terms = []
    for k in range(1, HALO + 1):
        if i - k < 0:
            terms.append((k, -1.0, low[HALO + i - k]))
        if i + k >= count:
            terms.append((k, 1.0, high[i + k - count]))
    return terms


def edge_slope(i, count, low, high):
    total = None
    for k, sign, value in edge_terms(i, count, low, high):
        term = (sign * C[k - 1]) * value
        total = term if total is None else total + term
    return total


def edge_laplace(i, count, low, high):
    total = None
    for k, _, value in edge_terms(i, count, low, high):
        term = A[k - 1] * value
        total = term if total is None else total + term
    return total


def depth_of_surface(topo_row, height):
    rows = lax.broadcasted_iota(jnp.int32, (height, height), 0)
    lanes = lax.broadcasted_iota(jnp.int32, (height, height), 1)
    picked = jnp.where(rows == lanes, topo_row.astype(F32), 0.0)
    return jnp.sum(picked, axis=1, keepdims=True).astype(jnp.int32)


def row_parity():
    return lax.rem(lax.axis_index("blk") // YBLOCKS, 2)


def column_parity():
    return lax.rem(lax.rem(lax.axis_index("blk"), YBLOCKS), 2)


def copy_all(pairs, sem):
    copies = [pltpu.make_async_copy(a, b, sem.at[n]) for n, (a, b) in enumerate(pairs)]
    for c in copies:
        c.start()
    return copies


def first_kernel(
    adj, mod, buoy, topo_in, fwd,
    x1, x2, f1, f2, y1, y2, s0,
    cur_v, mod_v, topo, buoy_v, fields_v, sem,
):
    width, height, depth = s0.shape
    parity = row_parity()
    first = pl.ds((1 - parity) * HALO, HALO)
    second = pl.ds(parity * HALO, HALO)
    copies = copy_all(
        [
            (topo_in, topo),
            (adj.at[0, 1, 0], cur_v),
            (mod.at[0], mod_v),
            (buoy.at[0], buoy_v),
            (fwd.at[0, pl.ds(1, 2), 0], fields_v),
            (buoy.at[0, first], x1.at[0]),
            (buoy.at[0, second], x2.at[0]),
            (fwd.at[0, pl.ds(1, 2), 0, first], f1),
            (fwd.at[0, pl.ds(1, 2), 0, second], f2),
        ],
        sem,
    )
    lanes = lax.broadcasted_iota(jnp.int32, (height, depth), 1)
    copies[0].wait()
    masks = [lanes >= depth_of_surface(topo[0, i : i + 1, :], height) for i in range(width)]
    copies[1].wait()
    copies[2].wait()
    for i in range(width):
        s0[i] = jnp.where(masks[i], mod_v[i] * cur_v[i], 0.0)
    x1[1] = s0[first]
    x2[1] = s0[second]
    even = column_parity() == 0

    def pack(n, value):
        low = value[:, :HALO]
        high = value[:, height - HALO :]
        y1[n] = jnp.where(even, high, low)
        y2[n] = jnp.where(even, low, high)

    pack(1, s0)
    copies[3].wait()
    pack(0, buoy_v)
    copies[4].wait()
    pack(2, fields_v.at[0])
    pack(3, fields_v.at[1])
    for c in copies[5:]:
        c.wait()


def early_kernel(
    adj, buoy, topo, s0, rec, res, y1, y2, zf, yf,
    rest, sx_own, sy, sz, gx_own, gy, gz, weight, scale, source,
    zs, zb, ys, yb,
):
    width, height, depth = s0.shape
    size = lax.axis_index("blk")
    anchor_x = size // YBLOCKS * width
    anchor_y = lax.rem(size, YBLOCKS) * height
    factor_y = yf[column_parity()]
    count = rec.shape[1]
    rx = rec[0:1, :] - anchor_x
    ry = rec[1:2, :] - anchor_y
    ids = lax.broadcasted_iota(jnp.int32, (STEPS * width, count), 0)
    values = jnp.concatenate(
        [jnp.broadcast_to(res[0, s : s + 1, :], (width, count)) for s in range(STEPS)], axis=0
    )
    hit_x = jnp.where(lax.rem(ids, width) == rx, values, 0.0)
    hit_y = (lax.broadcasted_iota(jnp.int32, (height, count), 0) == ry).astype(F32)
    plane = lax.dot_general(
        hit_y,
        hit_x,
        (((1,), (1,)), ((), ())),
        precision=lax.Precision.HIGHEST,
        preferred_element_type=F32,
    )
    zs[...] = z_product(s0[...], zf[...])
    zb[...] = z_product(buoy[0], zf[:, :depth])
    for i in range(width):
        ys[i] = y_product(s0[i], y1[1, i], y2[1, i], factor_y)
        yb[i] = y_product(buoy[0, i], y1[0, i], y2[0, i], factor_y[:height])
    lanes = lax.broadcasted_iota(jnp.int32, (height, depth), 1)
    for i in range(width):
        surface = depth_of_surface(topo[0, i : i + 1, :], height)
        live = lanes >= surface
        at = lanes == surface + 1
        scale[i] = jnp.where(live, TIME, 0.0)
        for s in range(STEPS):
            n = s * width + i
            source[s, i] = jnp.where(at, plane[:, n : n + 1], 0.0)
    for t in range(height // 8):
        rows = pl.ds(8 * t, 8)
        own = [s0[i, rows] for i in range(width)]
        slope = x_slope(own)
        laplace = x_laplace(own)
        for i in range(width):
            sx_own[i, rows] = slope[i]
            edge = ys[i, pl.ds(height + 8 * t, 8)] + zs[i, rows, depth:]
            laplace[i] = laplace[i] + A_UNIT * edge
        own = [buoy[0, i, rows] for i in range(width)]
        slope = x_slope(own)
        for i in range(width):
            w = scale[i, rows]
            gx_own[i, rows] = slope[i] * w
            g_y = (C_UNIT * w) * yb[i, rows]
            g_z = (C_UNIT * w) * zb[i, rows]
            s_y = C_UNIT * ys[i, rows]
            s_z = C_UNIT * zs[i, rows, :depth]
            b = own[i] * w
            weight[i, rows] = b
            gy[i, rows] = g_y
            gz[i, rows] = g_z
            sy[i, rows] = s_y
            sz[i, rows] = s_z
            moved = 2.0 * adj[0, 1, 0, i, rows] - adj[0, 0, 0, i, rows] + source[0, i, rows]
            moved = jnp.where(w > 0.0, moved, 0.0)
            rest[i, rows] = moved + b * laplace[i] + g_y * s_y + g_z * s_z


def finish_kernel(
    xa1, xa2, rest, sx_own, gx_own, weight, scale, mod,
    e0, s1, sx, gx, x1, x2, y2,
):
    width, height, depth = e0.shape

    def body(low_ref, high_ref, low_out, high_out):
        for t in range(height // 8):
            rows = pl.ds(8 * t, 8)
            low = [low_ref[1, i, rows] for i in range(HALO)]
            high = [high_ref[1, i, rows] for i in range(HALO)]
            low_b = [low_ref[0, i, rows] for i in range(HALO)]
            high_b = [high_ref[0, i, rows] for i in range(HALO)]
            for i in range(width):
                s_x = sx_own[i, rows] + edge_slope(i, width, low, high)
                g_x = gx_own[i, rows] + scale[i, rows] * edge_slope(i, width, low_b, high_b)
                earlier = (
                    rest[i, rows]
                    + weight[i, rows] * edge_laplace(i, width, low, high)
                    + g_x * s_x
                )
                scaled = mod[0, i, rows] * earlier
                sx[i, rows] = s_x
                gx[i, rows] = g_x
                e0[i, rows] = earlier
                s1[i, rows] = scaled
                if i < HALO:
                    low_out[i, rows] = scaled
                if i >= width - HALO:
                    high_out[i - (width - HALO), rows] = scaled

    @pl.when(row_parity() == 0)
    def _():
        body(xa2, xa1, x2, x1)

    @pl.when(row_parity() == 1)
    def _():
        body(xa1, xa2, x1, x2)

    even = column_parity() == 0
    y2[...] = jnp.where(even, s1[:, :HALO], s1[:, height - HALO :])


def middle_kernel(
    adj, e0, s1, sx0, sy0, sz0, gy, gz, weight, scale, source, fwd, xf1, xf2, yf1, yf2, zf, yf, ys2,
    rest, sx_own, image, fx, fy, y1, image_mod, states,
    zs, ys, z1, z2, ya, image_v, sem,
):
    width, height, depth = e0.shape
    first = pltpu.make_async_copy(e0, states.at[0, 0, 0], sem.at[0])
    first.start()
    even = column_parity() == 0
    y1[...] = jnp.where(even, s1[:, height - HALO :], s1[:, :HALO])
    for i in range(width):
        f0, f1, f2, f3 = (fwd[0, n, 0, i] for n in range(4))
        image_v[i] = adj[0, 1, 0, i] * (f0 - 2.0 * f1 + f2) + e0[i] * (f1 - 2.0 * f2 + f3)
    second = pltpu.make_async_copy(image_v, image_mod.at[0], sem.at[1])
    second.start()
    factor_y = yf[column_parity()]
    factor_own = factor_y[:, : 2 * height]
    zs[...] = z_product(s1[...], zf[...])
    z1[...] = z_product(fwd[0, 1, 0], zf[:, :depth])
    z2[...] = z_product(fwd[0, 2, 0], zf[:, :depth])
    for i in range(width):
        ys[i] = dot(factor_own, jnp.concatenate(parts(s1[i]), axis=0))
        ya[i] = y_product(fwd[0, 1, 0, i], yf1[2, i], yf2[2, i], factor_y[:height])
        fy[i] = y_product(fwd[0, 2, 0, i], yf1[3, i], yf2[3, i], factor_y[:height])

    def body(low_ref, high_ref):
        for t in range(height // 8):
            rows = pl.ds(8 * t, 8)
            own = [s1[i, rows] for i in range(width)]
            slope = x_slope(own)
            laplace = x_laplace(own)
            own1 = [fwd[0, 1, 0, i, rows] for i in range(width)]
            own2 = [fwd[0, 2, 0, i, rows] for i in range(width)]
            slope1 = x_slope(own1)
            slope2 = x_slope(own2)
            low1 = [low_ref[0, i, rows] for i in range(HALO)]
            high1 = [high_ref[0, i, rows] for i in range(HALO)]
            low2 = [low_ref[1, i, rows] for i in range(HALO)]
            high2 = [high_ref[1, i, rows] for i in range(HALO)]
            for i in range(width):
                now, before = adj[0, 1, 0, i, rows], e0[i, rows]
                s_y = C_UNIT * ys[i, rows]
                s_z = C_UNIT * zs[i, rows, :depth]
                edge = ys[i, pl.ds(height + 8 * t, 8)] + zs[i, rows, depth:]
                lap = laplace[i] + A_UNIT * edge
                moved = 2.0 * before - now + source[1, i, rows]
                moved = jnp.where(scale[i, rows] > 0.0, moved, 0.0)
                rest[i, rows] = (
                    moved + weight[i, rows] * lap + gy[i, rows] * s_y + gz[i, rows] * s_z
                )
                sx_own[i, rows] = slope[i]
                f1x = slope1[i] + edge_slope(i, width, low1, high1)
                fx[i, rows] = slope2[i] + edge_slope(i, width, low2, high2)
                image[i, rows] = (
                    f1x * sx0[i, rows]
                    + C_UNIT
                    * (
                        ya[i, rows] * sy0[i, rows]
                        + z1[i, rows] * sz0[i, rows]
                        + fy[i, rows] * s_y
                        + z2[i, rows] * s_z
                    )
                )

    @pl.when(row_parity() == 0)
    def _():
        body(xf2, xf1)

    @pl.when(row_parity() == 1)
    def _():
        body(xf1, xf2)

    first.wait()
    second.wait()


def last_kernel(
    xs1, xs2, ys1, ys2, rest, sx_own, image, fx, fy, gx, gy, weight, ye, states_in,
    image_out, states_out,
    image_v, e1_v, sem,
):
    width, height, depth = rest.shape
    tiles = height // 8
    factor = ye[column_parity()]

    def leave(t):
        rows = pl.ds(8 * t, 8)
        return (
            pltpu.make_async_copy(e1_v.at[:, rows], states_out.at[0, 1, 0, :, rows], sem.at[t]),
            pltpu.make_async_copy(image_v.at[:, rows], image_out.at[0, :, rows], sem.at[tiles + t]),
        )

    edges = [dot(factor, edge_parts(ys1[i], ys2[i])) for i in range(width)]

    def body(low_ref, high_ref):
        for t in range(tiles):
            rows = pl.ds(8 * t, 8)
            low = [low_ref[i, rows] for i in range(HALO)]
            high = [high_ref[i, rows] for i in range(HALO)]
            for i in range(width):
                s_x = sx_own[i, rows] + edge_slope(i, width, low, high)
                lap = edge_laplace(i, width, low, high)
                add = gx[i, rows] * s_x
                shown = fx[i, rows] * s_x
                if t == 0 or t == tiles - 1:
                    n = 0 if t == 0 else 8
                    s_y = C_UNIT * edges[i][n : n + 8]
                    lap = lap + A_UNIT * edges[i][16 + n : 24 + n]
                    add = add + gy[i, rows] * s_y
                    shown = shown + C_UNIT * (fy[i, rows] * s_y)
                e1_v[i, rows] = rest[i, rows] + weight[i, rows] * lap + add
                image_v[i, rows] = image[i, rows] + shown
            for c in leave(t):
                c.start()

    @pl.when(row_parity() == 0)
    def _():
        body(xs2, xs1)

    @pl.when(row_parity() == 1)
    def _():
        body(xs1, xs2)

    for t in range(tiles):
        for c in leave(t):
            c.wait()


def call(kernel, name, inputs, outputs, scratch=(), us=1.0, aliases=None):
    arrays, in_specs = [], []
    for array, near in inputs:
        place = VMEM if near else pltpu.HBM
        arrays.append(pltpu.with_memory_space_constraint(array, place))
        in_specs.append(pl.BlockSpec(memory_space=place))
    shapes, out_specs = [], []
    for shape, near in outputs:
        place = VMEM if near else pltpu.HBM
        shapes.append(place(shape, F32))
        out_specs.append(pl.BlockSpec(memory_space=place))
    return pl.pallas_call(
        kernel,
        name=name,
        in_specs=in_specs,
        out_specs=out_specs,
        out_shape=shapes,
        scratch_shapes=list(scratch),
        input_output_aliases=aliases or {},
        compiler_params=pltpu.CompilerParams(vmem_limit_bytes=16 * 1024 * 1024),
        cost_estimate=pl.CostEstimate(
            flops=0, bytes_accessed=int(us * 3.0e6), transcendentals=0
        ),
    )(*arrays)


def shards(adjoint_in, forward, modulus, buoyancy, topography, receivers, residuals):
    width, height, depth = modulus.shape[1:]
    block = (width, height, depth)
    size = lax.axis_size("blk")
    rows1, rows2 = row_pairs(size)
    cols1, cols2 = column_pairs(size)
    zf = jnp.asarray(along_z(depth), BF16)
    yf = jnp.asarray(along_y(height), BF16)
    ye = jnp.asarray(edge_rows(along_y(height), height), BF16)
    dma = pltpu.SemaphoreType.DMA

    def swap(value, pairs):
        return lax.ppermute(value, "blk", pairs)

    ahead = (2, HALO, height, depth)
    edge = (4, width, HALO, depth)
    xa1, xa2, xf1, xf2, ya1, ya2, s0 = call(
        first_kernel,
        "scaled_and_edges",
        [(adjoint_in, False), (modulus, False), (buoyancy, False), (topography, False), (forward, False)],
        [(ahead, True)] * 4 + [(edge, True)] * 2 + [(block, True)],
        [VMEM(block, F32), VMEM(block, F32), VMEM(topography.shape, jnp.int32), VMEM(block, F32),
         VMEM((2,) + block, F32), dma((9,))],
    )
    xa1, xa2 = swap(xa1, rows1), swap(xa2, rows2)
    ya1, ya2 = swap(ya1, cols1), swap(ya2, cols2)
    xf1, xf2 = swap(xf1, rows1), swap(xf2, rows2)
    z_out = (width, height, 2 * depth)
    y_out = (width, 2 * height, depth)
    rest, sx_own, sy, sz, gx_own, gy, gz, weight, scale, source = call(
        early_kernel,
        "step0_own",
        [(adjoint_in, True), (buoyancy, True), (topography, True), (s0, True),
         (receivers.T, True), (residuals, True), (ya1, True), (ya2, True), (zf, True), (yf, True)],
        [(block, True)] * 9 + [((STEPS,) + block, True)],
        [VMEM(z_out, F32), VMEM(block, F32), VMEM(y_out, F32), VMEM(block, F32)],
        us=4.0,
    )
    half = (HALO, height, depth)
    side = (width, HALO, depth)
    e0, s1, sx, gx, xs1, xs2, ys2 = call(
        finish_kernel,
        "step0_planes",
        [(xa1, True), (xa2, True), (rest, True), (sx_own, True), (gx_own, True), (weight, True), (scale, True),
         (modulus, True)],
        [(block, True)] * 4 + [(half, True)] * 2 + [(side, True)],
    )
    xs1, xs2, ys2 = swap(xs1, rows1), swap(xs2, rows2), swap(ys2, cols2)
    rest, sx_own, image, fx, fy, ys1, image_mod, states = call(
        middle_kernel,
        "images_and_step1_own",
        [(adjoint_in, True), (e0, True), (s1, True), (sx, True), (sy, True), (sz, True), (gy, True), (gz, True),
         (weight, True), (scale, True), (source, True), (forward, True), (xf1, True), (xf2, True), (ya1, True),
         (ya2, True), (zf, True), (yf, True), (ys2, True)],
        [(block, True)] * 5 + [(side, True), ((1,) + block, False), ((1, STEPS, 1) + block, False)],
        [VMEM(z_out, F32), VMEM(y_out, F32)] + [VMEM(block, F32)] * 4 + [dma((2,))],
        us=5.0,
    )
    ys1 = swap(ys1, cols1)
    image_buo, states = call(
        last_kernel,
        "step1_planes",
        [(xs1, True), (xs2, True), (ys1, True), (ys2, True), (rest, True), (sx_own, True), (image, True), (fx, True),
         (fy, True), (gx, True), (gy, True), (weight, True), (ye, True), (states, False)],
        [((1,) + block, False), ((1, STEPS, 1) + block, False)],
        [VMEM(block, F32), VMEM(block, F32), dma((2 * (height // 8),))],
        aliases={13: 1},
    )
    if lax.axis_size("shot") > 1:
        image_mod, image_buo = lax.psum((image_mod, image_buo), "shot")
    return image_mod, image_buo, states


def solution(mesh):
    placed = (
        P(("grp", "shot"), None, "blk", None, None, None),
        P(("grp", "shot"), None, "blk", None, None, None),
        P(("grp", "blk"), None, None, None),
        P(("grp", "blk"), None, None, None),
        P(("grp", "blk"), None, None),
        P("grp", None),
        P(("grp", "shot"), None, None),
    )
    return jax.shard_map(
        shards,
        mesh=mesh,
        in_specs=placed,
        out_specs=(
            P(("grp", "blk"), None, None, None),
            P(("grp", "blk"), None, None, None),
            P(("grp", "shot"), None, "blk", None, None, None),
        ),
        check_vma=False,
    )
```

```python
import numpy as np
import jax
import jax.numpy as jnp
from jax import lax
from jax.experimental import pallas as pl
from jax.experimental.pallas import tpu as pltpu
from jax.sharding import PartitionSpec as P

STEPS = 2
YBLOCKS = 4
HALO = 4

A0 = -205.0 / 72.0
A = (8.0 / 5.0, -1.0 / 5.0, 8.0 / 315.0, -1.0 / 560.0)
C = (4.0 / 5.0, -1.0 / 5.0, 4.0 / 105.0, -1.0 / 280.0)
A_INT = (8064.0, -1008.0, 128.0, -9.0)
C_INT = (672.0, -168.0, 32.0, -3.0)
A_UNIT = 1.0 / 5040.0
C_UNIT = 1.0 / 840.0
TIME = 0.03
F32 = jnp.float32
BF16 = jnp.bfloat16
VMEM = pltpu.VMEM


def row_pairs(size):
    first, second = [], []
    for i in range(size):
        r = i // YBLOCKS
        partner = i + YBLOCKS if r % 2 == 0 else i - YBLOCKS
        if 0 <= partner < size:
            first.append((i, partner))
        partner = i + YBLOCKS if r % 2 == 1 else i - YBLOCKS
        if 0 <= partner < size:
            second.append((i, partner))
    return first, second


def column_pairs(size):
    first, second = [], []
    for i in range(size):
        c = i % YBLOCKS
        partner = c + 1 if c % 2 == 0 else c - 1
        if 0 <= partner < YBLOCKS:
            first.append((i, i - c + partner))
        partner = c + 1 if c % 2 == 1 else c - 1
        if 0 <= partner < YBLOCKS:
            second.append((i, i - c + partner))
    return first, second


def along_z(depth):
    lap = np.zeros((depth, depth), np.float32)
    slope = np.zeros((depth, depth), np.float32)
    for k in range(1, HALO + 1):
        i = np.arange(depth - k)
        lap[i + k, i] += A_INT[k - 1]
        lap[i, i + k] += A_INT[k - 1]
        slope[i + k, i] += C_INT[k - 1]
        slope[i, i + k] -= C_INT[k - 1]
    return np.concatenate([slope, lap], axis=1)


def along_y(height):
    out = []
    for parity in range(2):
        full = np.zeros((2, height, height + 2 * HALO), np.float32)
        for i in range(height):
            for k in range(1, HALO + 1):
                full[0, i, HALO + i + k] += C_INT[k - 1]
                full[0, i, HALO + i - k] -= C_INT[k - 1]
                full[1, i, HALO + i + k] += A_INT[k - 1]
                full[1, i, HALO + i - k] += A_INT[k - 1]
        full = full.reshape(2 * height, height + 2 * HALO)
        low, own, high = full[:, :HALO], full[:, HALO:-HALO], full[:, -HALO:]
        edge = np.concatenate([high, low] if parity == 0 else [low, high], axis=1)
        out.append(np.concatenate([own, own, edge, edge], axis=1))
    return np.stack(out)


def edge_rows(factor, height):
    rows = np.concatenate([np.arange(8), np.arange(height - 8, height)])
    return factor[:, np.concatenate([rows, height + rows]), 2 * height :]


def parts(value):
    lead = value.astype(BF16)
    return lead, (value - lead.astype(F32)).astype(BF16)


def dot(a, b):
    return jnp.dot(a, b, preferred_element_type=F32)


def z_product(block, factor):
    planes, height, depth = block.shape
    lead, trail = parts(block.reshape(planes * height, depth))
    out = dot(lead, factor) + dot(trail, factor)
    return out.reshape(planes, height, out.shape[1])


def edge_parts(first, second):
    edge = jnp.concatenate([first, second], axis=0)
    lead = edge.astype(BF16).astype(F32)
    return jnp.concatenate([lead, edge - lead], axis=0).astype(BF16)


def y_product(plane, first, second, factor):
    lead, trail = parts(plane)
    return dot(factor, jnp.concatenate([lead, trail, edge_parts(first, second)], axis=0))


def x_slope(own):
    out = []
    for i in range(len(own)):
        total = None
        for k in range(1, HALO + 1):
            if i + k < len(own) and i - k >= 0:
                term = C[k - 1] * (own[i + k] - own[i - k])
            elif i + k < len(own):
                term = C[k - 1] * own[i + k]
            elif i - k >= 0:
                term = -C[k - 1] * own[i - k]
            else:
                continue
            total = term if total is None else total + term
        out.append(total)
    return out


def x_laplace(own):
    out = []
    for i in range(len(own)):
        total = 3.0 * A0 * own[i]
        for k in range(1, HALO + 1):
            if i + k < len(own) and i - k >= 0:
                total = total + A[k - 1] * (own[i + k] + own[i - k])
            elif i + k < len(own):
                total = total + A[k - 1] * own[i + k]
            elif i - k >= 0:
                total = total + A[k - 1] * own[i - k]
        out.append(total)
    return out


def edge_terms(i, count, low, high):
    terms = []
    for k in range(1, HALO + 1):
        if i - k < 0 and low is not None:
            terms.append((k, -1.0, low[HALO + i - k]))
        if i + k >= count and high is not None:
            terms.append((k, 1.0, high[i + k - count]))
    return terms


def edge_slope(i, count, low, high):
    total = None
    for k, sign, value in edge_terms(i, count, low, high):
        term = (sign * C[k - 1]) * value
        total = term if total is None else total + term
    return total


def plus(value, *terms):
    for term in terms:
        value = value if term is None else value + term
    return value


def edge_laplace(i, count, low, high):
    total = None
    for k, _, value in edge_terms(i, count, low, high):
        term = A[k - 1] * value
        total = term if total is None else total + term
    return total


def depth_of_surface(topo_row, height):
    rows = lax.broadcasted_iota(jnp.int32, (height, height), 0)
    lanes = lax.broadcasted_iota(jnp.int32, (height, height), 1)
    picked = jnp.where(rows == lanes, topo_row.astype(F32), 0.0)
    return jnp.sum(picked, axis=1, keepdims=True).astype(jnp.int32)


def planes(ref, n, rows):
    return None if ref is None else [ref[n, i, rows] for i in range(HALO)]


def row_parity():
    return lax.rem(lax.axis_index("blk") // YBLOCKS, 2)


def column_parity():
    return lax.rem(lax.rem(lax.axis_index("blk"), YBLOCKS), 2)


def copy_all(pairs, sem):
    copies = [pltpu.make_async_copy(a, b, sem.at[n]) for n, (a, b) in enumerate(pairs)]
    for c in copies:
        c.start()
    return copies


def first_kernel(
    adj, mod, buoy, topo_in, fwd,
    x1, x2, y1, y2, s0,
    cur_v, mod_v, topo, buoy_v, fields_v, sem,
):
    width, height, depth = s0.shape
    parity = row_parity()
    first = pl.ds((1 - parity) * HALO, HALO)
    second = pl.ds(parity * HALO, HALO)
    copies = copy_all(
        [
            (topo_in, topo),
            (adj.at[0, 1, 0], cur_v),
            (mod.at[0], mod_v),
            (buoy.at[0], buoy_v),
            (fwd.at[0, pl.ds(1, 2), 0], fields_v),
            (buoy.at[0, first], x1.at[0]),
            (buoy.at[0, second], x2.at[0]),
        ],
        sem,
    )
    lanes = lax.broadcasted_iota(jnp.int32, (height, depth), 1)
    copies[0].wait()
    masks = [lanes >= depth_of_surface(topo[0, i : i + 1, :], height) for i in range(width)]
    copies[1].wait()
    copies[2].wait()
    for i in range(width):
        s0[i] = jnp.where(masks[i], mod_v[i] * cur_v[i], 0.0)
    x1[1] = s0[first]
    x2[1] = s0[second]
    even = column_parity() == 0

    def pack(n, value):
        low = value[:, :HALO]
        high = value[:, height - HALO :]
        y1[n] = jnp.where(even, high, low)
        y2[n] = jnp.where(even, low, high)

    pack(1, s0)
    copies[3].wait()
    pack(0, buoy_v)
    copies[4].wait()
    pack(2, fields_v.at[0])
    pack(3, fields_v.at[1])
    for c in copies[5:]:
        c.wait()


def source_kernel(topo, rec, res, fwd, _, scale, source, x1, x2, sem):
    width, height, depth = scale.shape
    parity = row_parity()
    copies = copy_all(
        [
            (fwd.at[0, pl.ds(1, 2), 0, pl.ds((1 - parity) * HALO, HALO)], x1),
            (fwd.at[0, pl.ds(1, 2), 0, pl.ds(parity * HALO, HALO)], x2),
        ],
        sem,
    )
    index = lax.axis_index("blk")
    anchor_x = index // YBLOCKS * width
    anchor_y = lax.rem(index, YBLOCKS) * height
    count = rec.shape[1]
    rx = rec[0:1, :] - anchor_x
    ry = rec[1:2, :] - anchor_y
    ids = lax.broadcasted_iota(jnp.int32, (STEPS * width, count), 0)
    values = jnp.concatenate(
        [jnp.broadcast_to(res[0, s : s + 1, :], (width, count)) for s in range(STEPS)], axis=0
    )
    hit_x = jnp.where(lax.rem(ids, width) == rx, values, 0.0)
    hit_y = (lax.broadcasted_iota(jnp.int32, (height, count), 0) == ry).astype(F32)
    plane = lax.dot_general(
        hit_y,
        hit_x,
        (((1,), (1,)), ((), ())),
        precision=lax.Precision.HIGHEST,
        preferred_element_type=F32,
    )
    lanes = lax.broadcasted_iota(jnp.int32, (height, depth), 1)
    for i in range(width):
        surface = depth_of_surface(topo[0, i : i + 1, :], height)
        live = lanes >= surface
        at = lanes == surface + 1
        scale[i] = jnp.where(live, TIME, 0.0)
        for s in range(STEPS):
            n = s * width + i
            source[s, i] = jnp.where(at, plane[:, n : n + 1], 0.0)
    for c in copies:
        c.wait()


def early_kernel(
    adj, buoy, s0, y1, y2, zf, yf, scale, source,
    rest, sx_own, sy, sz, gx_own, gy, gz, weight,
    zs, zb, ys, yb,
):
    width, height, depth = s0.shape
    factor_y = yf[column_parity()]
    zs[...] = z_product(s0[...], zf[...])
    zb[...] = z_product(buoy[0], zf[:, :depth])
    for i in range(width):
        ys[i] = y_product(s0[i], y1[1, i], y2[1, i], factor_y)
        yb[i] = y_product(buoy[0, i], y1[0, i], y2[0, i], factor_y[:height])
    for t in range(height // 8):
        rows = pl.ds(8 * t, 8)
        own = [s0[i, rows] for i in range(width)]
        slope = x_slope(own)
        laplace = x_laplace(own)
        for i in range(width):
            sx_own[i, rows] = slope[i]
            edge = ys[i, pl.ds(height + 8 * t, 8)] + zs[i, rows, depth:]
            laplace[i] = laplace[i] + A_UNIT * edge
        own = [buoy[0, i, rows] for i in range(width)]
        slope = x_slope(own)
        for i in range(width):
            w = scale[i, rows]
            gx_own[i, rows] = slope[i] * w
            g_y = (C_UNIT * w) * yb[i, rows]
            g_z = (C_UNIT * w) * zb[i, rows]
            s_y = C_UNIT * ys[i, rows]
            s_z = C_UNIT * zs[i, rows, :depth]
            b = own[i] * w
            weight[i, rows] = b
            gy[i, rows] = g_y
            gz[i, rows] = g_z
            sy[i, rows] = s_y
            sz[i, rows] = s_z
            moved = 2.0 * adj[0, 1, 0, i, rows] - adj[0, 0, 0, i, rows] + source[0, i, rows]
            moved = jnp.where(w > 0.0, moved, 0.0)
            rest[i, rows] = moved + b * laplace[i] + g_y * s_y + g_z * s_z


def finish_kernel(
    xa1, xa2, rest, sx_own, gx_own, weight, scale, mod, _,
    e0, s1, sx, gx, x1, x2, y1, y2, f2,
):
    width, height, depth = e0.shape

    def body(low_ref, high_ref, low_out, high_out):
        for t in range(height // 8):
            rows = pl.ds(8 * t, 8)
            low = [low_ref[1, i, rows] for i in range(HALO)]
            high = [high_ref[1, i, rows] for i in range(HALO)]
            low_b = [low_ref[0, i, rows] for i in range(HALO)]
            high_b = [high_ref[0, i, rows] for i in range(HALO)]
            for i in range(width):
                s_x = sx_own[i, rows] + edge_slope(i, width, low, high)
                g_x = gx_own[i, rows] + scale[i, rows] * edge_slope(i, width, low_b, high_b)
                earlier = (
                    rest[i, rows]
                    + weight[i, rows] * edge_laplace(i, width, low, high)
                    + g_x * s_x
                )
                scaled = mod[0, i, rows] * earlier
                sx[i, rows] = s_x
                gx[i, rows] = g_x
                e0[i, rows] = earlier
                s1[i, rows] = scaled
                if i < HALO:
                    low_out[i, rows] = scaled
                if i >= width - HALO:
                    high_out[i - (width - HALO), rows] = scaled

    @pl.when(row_parity() == 0)
    def _():
        body(xa2, xa1, x2, x1)

    @pl.when(row_parity() == 1)
    def _():
        body(xa1, xa2, x1, x2)

    even = column_parity() == 0
    y1[...] = jnp.where(even, s1[:, height - HALO :], s1[:, :HALO])
    y2[...] = jnp.where(even, s1[:, :8], s1[:, height - 8 :])


def middle_kernel(
    adj, e0, s1, sx0, sy0, sz0, gy, gz, weight, scale, source, fwd, xf, yf1, yf2, zf, yf,
    rest, sx_own, image, fx, fy, image_mod, states,
    zs, ys, z1, z2, ya, image_v, sem,
):
    width, height, depth = e0.shape
    first = pltpu.make_async_copy(e0, states.at[0, 0, 0], sem.at[0])
    first.start()
    for i in range(width):
        f0, f1, f2, f3 = (fwd[0, n, 0, i] for n in range(4))
        image_v[i] = adj[0, 1, 0, i] * (f0 - 2.0 * f1 + f2) + e0[i] * (f1 - 2.0 * f2 + f3)
    second = pltpu.make_async_copy(image_v, image_mod.at[0], sem.at[1])
    second.start()
    factor_y = yf[column_parity()]
    factor_own = factor_y[:, : 2 * height]
    zs[...] = z_product(s1[...], zf[...])
    z1[...] = z_product(fwd[0, 1, 0], zf[:, :depth])
    z2[...] = z_product(fwd[0, 2, 0], zf[:, :depth])
    for i in range(width):
        ys[i] = dot(factor_own, jnp.concatenate(parts(s1[i]), axis=0))
        ya[i] = y_product(fwd[0, 1, 0, i], yf1[2, i], yf2[2, i], factor_y[:height])
        fy[i] = y_product(fwd[0, 2, 0, i], yf1[3, i], yf2[3, i], factor_y[:height])

    def body(low_ref, high_ref):
        for t in range(height // 8):
            rows = pl.ds(8 * t, 8)
            own = [s1[i, rows] for i in range(width)]
            slope = x_slope(own)
            laplace = x_laplace(own)
            own1 = [fwd[0, 1, 0, i, rows] for i in range(width)]
            own2 = [fwd[0, 2, 0, i, rows] for i in range(width)]
            slope1 = x_slope(own1)
            slope2 = x_slope(own2)
            low1, low2 = planes(low_ref, 0, rows), planes(low_ref, 1, rows)
            high1, high2 = planes(high_ref, 0, rows), planes(high_ref, 1, rows)
            for i in range(width):
                now, before = adj[0, 1, 0, i, rows], e0[i, rows]
                s_y = C_UNIT * ys[i, rows]
                s_z = C_UNIT * zs[i, rows, :depth]
                edge = ys[i, pl.ds(height + 8 * t, 8)] + zs[i, rows, depth:]
                lap = laplace[i] + A_UNIT * edge
                moved = 2.0 * before - now + source[1, i, rows]
                moved = jnp.where(scale[i, rows] > 0.0, moved, 0.0)
                rest[i, rows] = (
                    moved + weight[i, rows] * lap + gy[i, rows] * s_y + gz[i, rows] * s_z
                )
                sx_own[i, rows] = slope[i]
                f1x = plus(slope1[i], edge_slope(i, width, low1, high1))
                fx[i, rows] = plus(slope2[i], edge_slope(i, width, low2, high2))
                image[i, rows] = (
                    f1x * sx0[i, rows]
                    + C_UNIT
                    * (
                        ya[i, rows] * sy0[i, rows]
                        + z1[i, rows] * sz0[i, rows]
                        + fy[i, rows] * s_y
                        + z2[i, rows] * s_z
                    )
                )

    @pl.when(row_parity() == 0)
    def _():
        body(None, xf)

    @pl.when(row_parity() == 1)
    def _():
        body(xf, None)

    first.wait()
    second.wait()


def last_kernel(
    xs1, xs2, ys1, ys2, rest, sx_own, image, fx, fy, gx, gy, weight, ye, sx0, xf2, states_in,
    image_out, states_out,
    image_v, e1_v, sem,
):
    width, height, depth = rest.shape
    tiles = height // 8
    factor = ye[column_parity()]

    def leave(t):
        rows = pl.ds(8 * t, 8)
        return (
            pltpu.make_async_copy(e1_v.at[:, rows], states_out.at[0, 1, 0, :, rows], sem.at[t]),
            pltpu.make_async_copy(image_v.at[:, rows], image_out.at[0, :, rows], sem.at[tiles + t]),
        )

    even = column_parity() == 0
    edges = []
    for i in range(width):
        second = jnp.where(even, ys2[i, 8 - HALO :], ys2[i, :HALO])
        edges.append(dot(factor, edge_parts(ys1[i], second)))

    def body(low_ref, high_ref, low_fields, high_fields):
        for t in range(tiles):
            rows = pl.ds(8 * t, 8)
            low = [low_ref[i, rows] for i in range(HALO)]
            high = [high_ref[i, rows] for i in range(HALO)]
            low1, low2 = planes(low_fields, 0, rows), planes(low_fields, 1, rows)
            high1, high2 = planes(high_fields, 0, rows), planes(high_fields, 1, rows)
            for i in range(width):
                s_x = sx_own[i, rows] + edge_slope(i, width, low, high)
                lap = edge_laplace(i, width, low, high)
                add = gx[i, rows] * s_x
                f_x = plus(fx[i, rows], edge_slope(i, width, low2, high2))
                shown = image[i, rows] + f_x * s_x
                f_x = edge_slope(i, width, low1, high1)
                if f_x is not None:
                    shown = shown + f_x * sx0[i, rows]
                if t == 0 or t == tiles - 1:
                    n = 0 if t == 0 else 8
                    s_y = C_UNIT * edges[i][n : n + 8]
                    lap = lap + A_UNIT * edges[i][16 + n : 24 + n]
                    add = add + gy[i, rows] * s_y
                    shown = shown + C_UNIT * (fy[i, rows] * s_y)
                e1_v[i, rows] = rest[i, rows] + weight[i, rows] * lap + add
                image_v[i, rows] = shown
            for c in leave(t):
                c.start()

    @pl.when(row_parity() == 0)
    def _():
        body(xs2, xs1, xf2, None)

    @pl.when(row_parity() == 1)
    def _():
        body(xs1, xs2, None, xf2)

    for t in range(tiles):
        for c in leave(t):
            c.wait()


def call(kernel, name, inputs, outputs, scratch=(), us=1.0, aliases=None):
    arrays, in_specs = [], []
    for array, near in inputs:
        place = VMEM if near else pltpu.HBM
        arrays.append(pltpu.with_memory_space_constraint(array, place))
        in_specs.append(pl.BlockSpec(memory_space=place))
    shapes, out_specs = [], []
    for shape, near in outputs:
        place = VMEM if near else pltpu.HBM
        shapes.append(place(shape, F32))
        out_specs.append(pl.BlockSpec(memory_space=place))
    return pl.pallas_call(
        kernel,
        name=name,
        in_specs=in_specs,
        out_specs=out_specs,
        out_shape=shapes,
        scratch_shapes=list(scratch),
        input_output_aliases=aliases or {},
        compiler_params=pltpu.CompilerParams(vmem_limit_bytes=16 * 1024 * 1024),
        cost_estimate=pl.CostEstimate(
            flops=0, bytes_accessed=int(us * 3.0e6), transcendentals=0
        ),
    )(*arrays)


def shards(adjoint_in, forward, modulus, buoyancy, topography, receivers, residuals):
    width, height, depth = modulus.shape[1:]
    block = (width, height, depth)
    size = lax.axis_size("blk")
    rows1, rows2 = row_pairs(size)
    cols1, cols2 = column_pairs(size)
    zf = jnp.asarray(along_z(depth), BF16)
    yf = jnp.asarray(along_y(height), BF16)
    ye = jnp.asarray(edge_rows(along_y(height), height), BF16)
    dma = pltpu.SemaphoreType.DMA

    def swap(value, pairs):
        return lax.ppermute(value, "blk", pairs)

    ahead = (2, HALO, height, depth)
    edge = (4, width, HALO, depth)
    xa1, xa2, ya1, ya2, s0 = call(
        first_kernel,
        "scaled_and_edges",
        [(adjoint_in, False), (modulus, False), (buoyancy, False), (topography, False), (forward, False)],
        [(ahead, True)] * 2 + [(edge, True)] * 2 + [(block, True)],
        [VMEM(block, F32), VMEM(block, F32), VMEM(topography.shape, jnp.int32), VMEM(block, F32),
         VMEM((2,) + block, F32), dma((7,))],
    )
    xa1, xa2 = swap(xa1, rows1), swap(xa2, rows2)
    ya1, ya2 = swap(ya1, cols1), swap(ya2, cols2)
    z_out = (width, height, 2 * depth)
    y_out = (width, 2 * height, depth)
    scale, source, xf1, xf2 = call(
        source_kernel,
        "sources_and_planes",
        [(topography, True), (receivers.T, True), (residuals, True), (forward, False), (ya1, True)],
        [(block, True), ((STEPS,) + block, True), (ahead, True), (ahead, True)],
        [dma((2,))],
    )
    xf1 = swap(xf1, rows1)
    rest, sx_own, sy, sz, gx_own, gy, gz, weight = call(
        early_kernel,
        "step0_own",
        [(adjoint_in, True), (buoyancy, True), (s0, True), (ya1, True), (ya2, True), (zf, True), (yf, True),
         (scale, True), (source, True)],
        [(block, True)] * 8,
        [VMEM(z_out, F32), VMEM(block, F32), VMEM(y_out, F32), VMEM(block, F32)],
        us=4.0,
    )
    half = (HALO, height, depth)
    side = (width, HALO, depth)
    rows8 = (width, 8, depth)
    e0, s1, sx, gx, xs1, xs2, ys1, ys2, xf2 = call(
        finish_kernel,
        "step0_planes",
        [(xa1, True), (xa2, True), (rest, True), (sx_own, True), (gx_own, True), (weight, True), (scale, True),
         (modulus, True), (xf2, True)],
        [(block, True)] * 4 + [(half, True)] * 2 + [(side, True), (rows8, True)] + [(ahead, True)],
        aliases={8: 8},
    )
    xf2, xs1, xs2 = swap(xf2, rows2), swap(xs1, rows1), swap(xs2, rows2)
    ys1, ys2 = swap(ys1, cols1), swap(ys2, cols2)
    rest, sx_own, image, fx, fy, image_mod, states = call(
        middle_kernel,
        "images_and_step1_own",
        [(adjoint_in, True), (e0, True), (s1, True), (sx, True), (sy, True), (sz, True), (gy, True), (gz, True),
         (weight, True), (scale, True), (source, True), (forward, True), (xf1, True), (ya1, True),
         (ya2, True), (zf, True), (yf, True)],
        [(block, True)] * 5 + [((1,) + block, False), ((1, STEPS, 1) + block, False)],
        [VMEM(z_out, F32), VMEM(y_out, F32)] + [VMEM(block, F32)] * 4 + [dma((2,))],
        us=20.0,
    )
    image_buo, states = call(
        last_kernel,
        "step1_planes",
        [(xs1, True), (xs2, True), (ys1, True), (ys2, True), (rest, True), (sx_own, True), (image, True), (fx, True),
         (fy, True), (gx, True), (gy, True), (weight, True), (ye, True), (sx, True), (xf2, True), (states, False)],
        [((1,) + block, False), ((1, STEPS, 1) + block, False)],
        [VMEM(block, F32), VMEM(block, F32), dma((2 * (height // 8),))],
        aliases={15: 1},
    )
    if lax.axis_size("shot") > 1:
        image_mod, image_buo = lax.psum((image_mod, image_buo), "shot")
    return image_mod, image_buo, states


def solution(mesh):
    placed = (
        P(("grp", "shot"), None, "blk", None, None, None),
        P(("grp", "shot"), None, "blk", None, None, None),
        P(("grp", "blk"), None, None, None),
        P(("grp", "blk"), None, None, None),
        P(("grp", "blk"), None, None),
        P("grp", None),
        P(("grp", "shot"), None, None),
    )
    return jax.shard_map(
        shards,
        mesh=mesh,
        in_specs=placed,
        out_specs=(
            P(("grp", "blk"), None, None, None),
            P(("grp", "blk"), None, None, None),
            P(("grp", "shot"), None, "blk", None, None, None),
        ),
        check_vma=False,
    )
```

```python
import numpy as np
import jax
import jax.numpy as jnp
from jax import lax
from jax.experimental import pallas as pl
from jax.experimental.pallas import tpu as pltpu
from jax.sharding import PartitionSpec as P

STEPS = 2
YBLOCKS = 4
HALO = 4

A0 = -205.0 / 72.0
A = (8.0 / 5.0, -1.0 / 5.0, 8.0 / 315.0, -1.0 / 560.0)
C = (4.0 / 5.0, -1.0 / 5.0, 4.0 / 105.0, -1.0 / 280.0)
A_INT = (8064.0, -1008.0, 128.0, -9.0)
C_INT = (672.0, -168.0, 32.0, -3.0)
A_UNIT = 1.0 / 5040.0
C_UNIT = 1.0 / 840.0
TIME = 0.03
F32 = jnp.float32
BF16 = jnp.bfloat16
VMEM = pltpu.VMEM


def row_pairs(size):
    first, second = [], []
    for i in range(size):
        r = i // YBLOCKS
        partner = i + YBLOCKS if r % 2 == 0 else i - YBLOCKS
        if 0 <= partner < size:
            first.append((i, partner))
        partner = i + YBLOCKS if r % 2 == 1 else i - YBLOCKS
        if 0 <= partner < size:
            second.append((i, partner))
    return first, second


def column_pairs(size):
    first, second = [], []
    for i in range(size):
        c = i % YBLOCKS
        partner = c + 1 if c % 2 == 0 else c - 1
        if 0 <= partner < YBLOCKS:
            first.append((i, i - c + partner))
        partner = c + 1 if c % 2 == 1 else c - 1
        if 0 <= partner < YBLOCKS:
            second.append((i, i - c + partner))
    return first, second


def along_z(depth):
    lap = np.zeros((depth, depth), np.float32)
    slope = np.zeros((depth, depth), np.float32)
    for k in range(1, HALO + 1):
        i = np.arange(depth - k)
        lap[i + k, i] += A_INT[k - 1]
        lap[i, i + k] += A_INT[k - 1]
        slope[i + k, i] += C_INT[k - 1]
        slope[i, i + k] -= C_INT[k - 1]
    return np.concatenate([slope, lap], axis=1)


def along_y(height):
    out = []
    for parity in range(2):
        full = np.zeros((2, height, height + 2 * HALO), np.float32)
        for i in range(height):
            for k in range(1, HALO + 1):
                full[0, i, HALO + i + k] += C_INT[k - 1]
                full[0, i, HALO + i - k] -= C_INT[k - 1]
                full[1, i, HALO + i + k] += A_INT[k - 1]
                full[1, i, HALO + i - k] += A_INT[k - 1]
        full = full.reshape(2 * height, height + 2 * HALO)
        low, own, high = full[:, :HALO], full[:, HALO:-HALO], full[:, -HALO:]
        edge = np.concatenate([high, low] if parity == 0 else [low, high], axis=1)
        out.append(np.concatenate([own, own, edge, edge], axis=1))
    return np.stack(out)


def edge_rows(factor, height):
    rows = np.concatenate([np.arange(8), np.arange(height - 8, height)])
    return factor[:, np.concatenate([rows, height + rows]), 2 * height :]


def parts(value):
    lead = value.astype(BF16)
    return lead, (value - lead.astype(F32)).astype(BF16)


def dot(a, b):
    return jnp.dot(a, b, preferred_element_type=F32)


def z_product(block, factor):
    planes, height, depth = block.shape
    lead, trail = parts(block.reshape(planes * height, depth))
    out = dot(lead, factor) + dot(trail, factor)
    return out.reshape(planes, height, out.shape[1])


def edge_parts(first, second):
    edge = jnp.concatenate([first, second], axis=0)
    lead = edge.astype(BF16).astype(F32)
    return jnp.concatenate([lead, edge - lead], axis=0).astype(BF16)


def y_product(plane, first, second, factor):
    lead, trail = parts(plane)
    return dot(factor, jnp.concatenate([lead, trail, edge_parts(first, second)], axis=0))


def x_slope(own):
    out = []
    for i in range(len(own)):
        total = None
        for k in range(1, HALO + 1):
            if i + k < len(own) and i - k >= 0:
                term = C[k - 1] * (own[i + k] - own[i - k])
            elif i + k < len(own):
                term = C[k - 1] * own[i + k]
            elif i - k >= 0:
                term = -C[k - 1] * own[i - k]
            else:
                continue
            total = term if total is None else total + term
        out.append(total)
    return out


def x_laplace(own):
    out = []
    for i in range(len(own)):
        total = 3.0 * A0 * own[i]
        for k in range(1, HALO + 1):
            if i + k < len(own) and i - k >= 0:
                total = total + A[k - 1] * (own[i + k] + own[i - k])
            elif i + k < len(own):
                total = total + A[k - 1] * own[i + k]
            elif i - k >= 0:
                total = total + A[k - 1] * own[i - k]
        out.append(total)
    return out


def edge_terms(i, count, low, high):
    terms = []
    for k in range(1, HALO + 1):
        if i - k < 0 and low is not None:
            terms.append((k, -1.0, low[HALO + i - k]))
        if i + k >= count and high is not None:
            terms.append((k, 1.0, high[i + k - count]))
    return terms


def edge_slope(i, count, low, high):
    total = None
    for k, sign, value in edge_terms(i, count, low, high):
        term = (sign * C[k - 1]) * value
        total = term if total is None else total + term
    return total


def plus(value, *terms):
    for term in terms:
        value = value if term is None else value + term
    return value


def edge_laplace(i, count, low, high):
    total = None
    for k, _, value in edge_terms(i, count, low, high):
        term = A[k - 1] * value
        total = term if total is None else total + term
    return total


def depth_of_surface(topo_row, height):
    rows = lax.broadcasted_iota(jnp.int32, (height, height), 0)
    lanes = lax.broadcasted_iota(jnp.int32, (height, height), 1)
    picked = jnp.where(rows == lanes, topo_row.astype(F32), 0.0)
    return jnp.sum(picked, axis=1, keepdims=True).astype(jnp.int32)


def planes(ref, n, rows):
    return None if ref is None else [ref[n, i, rows] for i in range(HALO)]


def row_parity():
    return lax.rem(lax.axis_index("blk") // YBLOCKS, 2)


def column_parity():
    return lax.rem(lax.rem(lax.axis_index("blk"), YBLOCKS), 2)


def copy_all(pairs, sem):
    copies = [pltpu.make_async_copy(a, b, sem.at[n]) for n, (a, b) in enumerate(pairs)]
    for c in copies:
        c.start()
    return copies


def first_kernel(adj, mod, buoy, topo_in, x1, x2, s0, cur_v, mod_v, topo, sem):
    width, height, depth = s0.shape
    parity = row_parity()
    first = pl.ds((1 - parity) * HALO, HALO)
    second = pl.ds(parity * HALO, HALO)
    copies = copy_all(
        [
            (topo_in, topo),
            (adj.at[0, 1, 0], cur_v),
            (mod.at[0], mod_v),
            (buoy.at[0, first], x1.at[0]),
            (buoy.at[0, second], x2.at[0]),
        ],
        sem,
    )
    lanes = lax.broadcasted_iota(jnp.int32, (height, depth), 1)
    copies[0].wait()
    masks = [lanes >= depth_of_surface(topo[0, i : i + 1, :], height) for i in range(width)]
    copies[1].wait()
    copies[2].wait()
    for i in range(width):
        s0[i] = jnp.where(masks[i], mod_v[i] * cur_v[i], 0.0)
    x1[1] = s0[first]
    x2[1] = s0[second]
    for c in copies[3:]:
        c.wait()


def edge_kernel(buoy, fwd, s0, y1, y2, low_v, high_v, sem):
    width, height, depth = s0.shape
    low, high = pl.ds(0, 8), pl.ds(height - 8, 8)
    copies = copy_all(
        [
            (buoy.at[0, :, low], low_v.at[0]),
            (buoy.at[0, :, high], high_v.at[0]),
            (fwd.at[0, pl.ds(1, 2), 0, :, low], low_v.at[pl.ds(1, 2)]),
            (fwd.at[0, pl.ds(1, 2), 0, :, high], high_v.at[pl.ds(1, 2)]),
        ],
        sem,
    )
    even = column_parity() == 0

    def pack(n, low, high):
        y1[n] = jnp.where(even, high, low)
        y2[n] = jnp.where(even, low, high)

    pack(1, s0[:, :HALO], s0[:, height - HALO :])
    for c in copies:
        c.wait()
    for n, m in ((0, 0), (2, 1), (3, 2)):
        pack(n, low_v[m, :, :HALO], high_v[m, :, 8 - HALO :])


def source_kernel(topo, rec, res, fwd, _, scale, source, x1, x2, sem):
    width, height, depth = scale.shape
    parity = row_parity()
    copies = copy_all(
        [
            (fwd.at[0, pl.ds(1, 2), 0, pl.ds((1 - parity) * HALO, HALO)], x1),
            (fwd.at[0, pl.ds(1, 2), 0, pl.ds(parity * HALO, HALO)], x2),
        ],
        sem,
    )
    index = lax.axis_index("blk")
    anchor_x = index // YBLOCKS * width
    anchor_y = lax.rem(index, YBLOCKS) * height
    count = rec.shape[1]
    rx = rec[0:1, :] - anchor_x
    ry = rec[1:2, :] - anchor_y
    ids = lax.broadcasted_iota(jnp.int32, (STEPS * width, count), 0)
    values = jnp.concatenate(
        [jnp.broadcast_to(res[0, s : s + 1, :], (width, count)) for s in range(STEPS)], axis=0
    )
    hit_x = jnp.where(lax.rem(ids, width) == rx, values, 0.0)
    hit_y = (lax.broadcasted_iota(jnp.int32, (height, count), 0) == ry).astype(F32)
    plane = lax.dot_general(
        hit_y,
        hit_x,
        (((1,), (1,)), ((), ())),
        precision=lax.Precision.HIGHEST,
        preferred_element_type=F32,
    )
    lanes = lax.broadcasted_iota(jnp.int32, (height, depth), 1)
    for i in range(width):
        surface = depth_of_surface(topo[0, i : i + 1, :], height)
        live = lanes >= surface
        at = lanes == surface + 1
        scale[i] = jnp.where(live, TIME, 0.0)
        for s in range(STEPS):
            n = s * width + i
            source[s, i] = jnp.where(at, plane[:, n : n + 1], 0.0)
    for c in copies:
        c.wait()


def early_kernel(
    adj, buoy, s0, y1, y2, zf, yf, scale, source,
    rest, sx_own, sy, sz, gx_own, gy, gz, weight,
    zs, zb, ys, yb,
):
    width, height, depth = s0.shape
    factor_y = yf[column_parity()]
    zs[...] = z_product(s0[...], zf[...])
    zb[...] = z_product(buoy[0], zf[:, :depth])
    for i in range(width):
        ys[i] = y_product(s0[i], y1[1, i], y2[1, i], factor_y)
        yb[i] = y_product(buoy[0, i], y1[0, i], y2[0, i], factor_y[:height])
    for t in range(height // 8):
        rows = pl.ds(8 * t, 8)
        own = [s0[i, rows] for i in range(width)]
        slope = x_slope(own)
        laplace = x_laplace(own)
        for i in range(width):
            sx_own[i, rows] = slope[i]
            edge = ys[i, pl.ds(height + 8 * t, 8)] + zs[i, rows, depth:]
            laplace[i] = laplace[i] + A_UNIT * edge
        own = [buoy[0, i, rows] for i in range(width)]
        slope = x_slope(own)
        for i in range(width):
            w = scale[i, rows]
            gx_own[i, rows] = slope[i] * w
            g_y = (C_UNIT * w) * yb[i, rows]
            g_z = (C_UNIT * w) * zb[i, rows]
            s_y = C_UNIT * ys[i, rows]
            s_z = C_UNIT * zs[i, rows, :depth]
            b = own[i] * w
            weight[i, rows] = b
            gy[i, rows] = g_y
            gz[i, rows] = g_z
            sy[i, rows] = s_y
            sz[i, rows] = s_z
            moved = 2.0 * adj[0, 1, 0, i, rows] - adj[0, 0, 0, i, rows] + source[0, i, rows]
            moved = jnp.where(w > 0.0, moved, 0.0)
            rest[i, rows] = moved + b * laplace[i] + g_y * s_y + g_z * s_z


def finish_kernel(
    xa1, xa2, rest, sx_own, gx_own, weight, scale, mod, _,
    e0, s1, sx, gx, x1, x2, y1, y2, f2,
):
    width, height, depth = e0.shape

    def body(low_ref, high_ref, low_out, high_out):
        for t in range(height // 8):
            rows = pl.ds(8 * t, 8)
            low = [low_ref[1, i, rows] for i in range(HALO)]
            high = [high_ref[1, i, rows] for i in range(HALO)]
            low_b = [low_ref[0, i, rows] for i in range(HALO)]
            high_b = [high_ref[0, i, rows] for i in range(HALO)]
            for i in range(width):
                s_x = sx_own[i, rows] + edge_slope(i, width, low, high)
                g_x = gx_own[i, rows] + scale[i, rows] * edge_slope(i, width, low_b, high_b)
                earlier = (
                    rest[i, rows]
                    + weight[i, rows] * edge_laplace(i, width, low, high)
                    + g_x * s_x
                )
                scaled = mod[0, i, rows] * earlier
                sx[i, rows] = s_x
                gx[i, rows] = g_x
                e0[i, rows] = earlier
                s1[i, rows] = scaled
                if i < HALO:
                    low_out[i, rows] = scaled
                if i >= width - HALO:
                    high_out[i - (width - HALO), rows] = scaled

    @pl.when(row_parity() == 0)
    def _():
        body(xa2, xa1, x2, x1)

    @pl.when(row_parity() == 1)
    def _():
        body(xa1, xa2, x1, x2)

    even = column_parity() == 0
    y1[...] = jnp.where(even, s1[:, height - HALO :], s1[:, :HALO])
    y2[...] = jnp.where(even, s1[:, :8], s1[:, height - 8 :])


def middle_kernel(
    adj, e0, s1, sx0, sy0, sz0, gy, gz, weight, scale, source, fwd, xf, yf1, yf2, zf, yf,
    rest, sx_own, image, fx, fy, image_mod, states,
    zs, ys, z1, z2, ya, image_v, sem,
):
    width, height, depth = e0.shape
    first = pltpu.make_async_copy(e0, states.at[0, 0, 0], sem.at[0])
    first.start()
    for i in range(width):
        f0, f1, f2, f3 = (fwd[0, n, 0, i] for n in range(4))
        image_v[i] = adj[0, 1, 0, i] * (f0 - 2.0 * f1 + f2) + e0[i] * (f1 - 2.0 * f2 + f3)
    second = pltpu.make_async_copy(image_v, image_mod.at[0], sem.at[1])
    second.start()
    factor_y = yf[column_parity()]
    factor_own = factor_y[:, : 2 * height]
    zs[...] = z_product(s1[...], zf[...])
    z1[...] = z_product(fwd[0, 1, 0], zf[:, :depth])
    z2[...] = z_product(fwd[0, 2, 0], zf[:, :depth])
    for i in range(width):
        ys[i] = dot(factor_own, jnp.concatenate(parts(s1[i]), axis=0))
        ya[i] = y_product(fwd[0, 1, 0, i], yf1[2, i], yf2[2, i], factor_y[:height])
        fy[i] = y_product(fwd[0, 2, 0, i], yf1[3, i], yf2[3, i], factor_y[:height])

    def body(low_ref, high_ref):
        for t in range(height // 8):
            rows = pl.ds(8 * t, 8)
            own = [s1[i, rows] for i in range(width)]
            slope = x_slope(own)
            laplace = x_laplace(own)
            own1 = [fwd[0, 1, 0, i, rows] for i in range(width)]
            own2 = [fwd[0, 2, 0, i, rows] for i in range(width)]
            slope1 = x_slope(own1)
            slope2 = x_slope(own2)
            low1, low2 = planes(low_ref, 0, rows), planes(low_ref, 1, rows)
            high1, high2 = planes(high_ref, 0, rows), planes(high_ref, 1, rows)
            for i in range(width):
                now, before = adj[0, 1, 0, i, rows], e0[i, rows]
                s_y = C_UNIT * ys[i, rows]
                s_z = C_UNIT * zs[i, rows, :depth]
                edge = ys[i, pl.ds(height + 8 * t, 8)] + zs[i, rows, depth:]
                lap = laplace[i] + A_UNIT * edge
                moved = 2.0 * before - now + source[1, i, rows]
                moved = jnp.where(scale[i, rows] > 0.0, moved, 0.0)
                rest[i, rows] = (
                    moved + weight[i, rows] * lap + gy[i, rows] * s_y + gz[i, rows] * s_z
                )
                sx_own[i, rows] = slope[i]
                f1x = plus(slope1[i], edge_slope(i, width, low1, high1))
                fx[i, rows] = plus(slope2[i], edge_slope(i, width, low2, high2))
                image[i, rows] = (
                    f1x * sx0[i, rows]
                    + C_UNIT
                    * (
                        ya[i, rows] * sy0[i, rows]
                        + z1[i, rows] * sz0[i, rows]
                        + fy[i, rows] * s_y
                        + z2[i, rows] * s_z
                    )
                )

    @pl.when(row_parity() == 0)
    def _():
        body(None, xf)

    @pl.when(row_parity() == 1)
    def _():
        body(xf, None)

    first.wait()
    second.wait()


def last_kernel(
    xs1, xs2, ys1, ys2, rest, sx_own, image, fx, fy, gx, gy, weight, ye, sx0, xf2, states_in,
    image_out, states_out,
    image_v, e1_v, sem,
):
    width, height, depth = rest.shape
    tiles = height // 8
    factor = ye[column_parity()]

    def leave(t):
        rows = pl.ds(8 * t, 8)
        return (
            pltpu.make_async_copy(e1_v.at[:, rows], states_out.at[0, 1, 0, :, rows], sem.at[t]),
            pltpu.make_async_copy(image_v.at[:, rows], image_out.at[0, :, rows], sem.at[tiles + t]),
        )

    even = column_parity() == 0

    def edge_of(i):
        second = jnp.where(even, ys2[i, 8 - HALO :], ys2[i, :HALO])
        return dot(factor, edge_parts(ys1[i], second))

    def body(low_ref, high_ref, low_fields, high_fields):
        edges = [edge_of(i) for i in range(width)]
        for t in list(range(1, tiles - 1)) + [0, tiles - 1]:
            rows = pl.ds(8 * t, 8)
            low = [low_ref[i, rows] for i in range(HALO)]
            high = [high_ref[i, rows] for i in range(HALO)]
            low1, low2 = planes(low_fields, 0, rows), planes(low_fields, 1, rows)
            high1, high2 = planes(high_fields, 0, rows), planes(high_fields, 1, rows)
            for i in range(width):
                s_x = sx_own[i, rows] + edge_slope(i, width, low, high)
                lap = edge_laplace(i, width, low, high)
                add = gx[i, rows] * s_x
                f_x = plus(fx[i, rows], edge_slope(i, width, low2, high2))
                shown = image[i, rows] + f_x * s_x
                f_x = edge_slope(i, width, low1, high1)
                if f_x is not None:
                    shown = shown + f_x * sx0[i, rows]
                if t == 0 or t == tiles - 1:
                    n = 0 if t == 0 else 8
                    s_y = C_UNIT * edges[i][n : n + 8]
                    lap = lap + A_UNIT * edges[i][16 + n : 24 + n]
                    add = add + gy[i, rows] * s_y
                    shown = shown + C_UNIT * (fy[i, rows] * s_y)
                e1_v[i, rows] = rest[i, rows] + weight[i, rows] * lap + add
                image_v[i, rows] = shown
            for c in leave(t):
                c.start()

    @pl.when(row_parity() == 0)
    def _():
        body(xs2, xs1, xf2, None)

    @pl.when(row_parity() == 1)
    def _():
        body(xs1, xs2, None, xf2)

    for t in range(tiles):
        for c in leave(t):
            c.wait()


def call(kernel, name, inputs, outputs, scratch=(), us=1.0, aliases=None):
    arrays, in_specs = [], []
    for array, near in inputs:
        place = VMEM if near else pltpu.HBM
        arrays.append(pltpu.with_memory_space_constraint(array, place))
        in_specs.append(pl.BlockSpec(memory_space=place))
    shapes, out_specs = [], []
    for shape, near in outputs:
        place = VMEM if near else pltpu.HBM
        shapes.append(place(shape, F32))
        out_specs.append(pl.BlockSpec(memory_space=place))
    return pl.pallas_call(
        kernel,
        name=name,
        in_specs=in_specs,
        out_specs=out_specs,
        out_shape=shapes,
        scratch_shapes=list(scratch),
        input_output_aliases=aliases or {},
        compiler_params=pltpu.CompilerParams(vmem_limit_bytes=16 * 1024 * 1024),
        cost_estimate=pl.CostEstimate(
            flops=0, bytes_accessed=int(us * 3.0e6), transcendentals=0
        ),
    )(*arrays)


def shards(adjoint_in, forward, modulus, buoyancy, topography, receivers, residuals):
    width, height, depth = modulus.shape[1:]
    block = (width, height, depth)
    size = lax.axis_size("blk")
    rows1, rows2 = row_pairs(size)
    cols1, cols2 = column_pairs(size)
    zf = jnp.asarray(along_z(depth), BF16)
    yf = jnp.asarray(along_y(height), BF16)
    ye = jnp.asarray(edge_rows(along_y(height), height), BF16)
    dma = pltpu.SemaphoreType.DMA

    def swap(value, pairs):
        return lax.ppermute(value, "blk", pairs)

    ahead = (2, HALO, height, depth)
    edge = (4, width, HALO, depth)
    xa1, xa2, s0 = call(
        first_kernel,
        "scaled_and_planes",
        [(adjoint_in, False), (modulus, False), (buoyancy, False), (topography, False)],
        [(ahead, True)] * 2 + [(block, True)],
        [VMEM(block, F32), VMEM(block, F32), VMEM(topography.shape, jnp.int32), dma((5,))],
    )
    xa1, xa2 = swap(xa1, rows1), swap(xa2, rows2)
    ya1, ya2 = call(
        edge_kernel,
        "edges",
        [(buoyancy, False), (forward, False), (s0, True)],
        [(edge, True)] * 2,
        [VMEM((3, width, 8, depth), F32), VMEM((3, width, 8, depth), F32), dma((4,))],
    )
    ya1, ya2 = swap(ya1, cols1), swap(ya2, cols2)
    z_out = (width, height, 2 * depth)
    y_out = (width, 2 * height, depth)
    scale, source, xf1, xf2 = call(
        source_kernel,
        "sources_and_planes",
        [(topography, True), (receivers.T, True), (residuals, True), (forward, False), (ya1, True)],
        [(block, True), ((STEPS,) + block, True), (ahead, True), (ahead, True)],
        [dma((2,))],
    )
    xf1 = swap(xf1, rows1)
    rest, sx_own, sy, sz, gx_own, gy, gz, weight = call(
        early_kernel,
        "step0_own",
        [(adjoint_in, True), (buoyancy, True), (s0, True), (ya1, True), (ya2, True), (zf, True), (yf, True),
         (scale, True), (source, True)],
        [(block, True)] * 8,
        [VMEM(z_out, F32), VMEM(block, F32), VMEM(y_out, F32), VMEM(block, F32)],
        us=4.0,
    )
    half = (HALO, height, depth)
    side = (width, HALO, depth)
    rows8 = (width, 8, depth)
    e0, s1, sx, gx, xs1, xs2, ys1, ys2, xf2 = call(
        finish_kernel,
        "step0_planes",
        [(xa1, True), (xa2, True), (rest, True), (sx_own, True), (gx_own, True), (weight, True), (scale, True),
         (modulus, True), (xf2, True)],
        [(block, True)] * 4 + [(half, True)] * 2 + [(side, True), (rows8, True)] + [(ahead, True)],
        aliases={8: 8},
    )
    xf2, xs1, xs2 = swap(xf2, rows2), swap(xs1, rows1), swap(xs2, rows2)
    ys1, ys2 = swap(ys1, cols1), swap(ys2, cols2)
    rest, sx_own, image, fx, fy, image_mod, states = call(
        middle_kernel,
        "images_and_step1_own",
        [(adjoint_in, True), (e0, True), (s1, True), (sx, True), (sy, True), (sz, True), (gy, True), (gz, True),
         (weight, True), (scale, True), (source, True), (forward, True), (xf1, True), (ya1, True),
         (ya2, True), (zf, True), (yf, True)],
        [(block, True)] * 5 + [((1,) + block, False), ((1, STEPS, 1) + block, False)],
        [VMEM(z_out, F32), VMEM(y_out, F32)] + [VMEM(block, F32)] * 4 + [dma((2,))],
        us=20.0,
    )
    image_buo, states = call(
        last_kernel,
        "step1_planes",
        [(xs1, True), (xs2, True), (ys1, True), (ys2, True), (rest, True), (sx_own, True), (image, True), (fx, True),
         (fy, True), (gx, True), (gy, True), (weight, True), (ye, True), (sx, True), (xf2, True), (states, False)],
        [((1,) + block, False), ((1, STEPS, 1) + block, False)],
        [VMEM(block, F32), VMEM(block, F32), dma((2 * (height // 8),))],
        aliases={15: 1},
    )
    if lax.axis_size("shot") > 1:
        image_mod, image_buo = lax.psum((image_mod, image_buo), "shot")
    return image_mod, image_buo, states


def solution(mesh):
    placed = (
        P(("grp", "shot"), None, "blk", None, None, None),
        P(("grp", "shot"), None, "blk", None, None, None),
        P(("grp", "blk"), None, None, None),
        P(("grp", "blk"), None, None, None),
        P(("grp", "blk"), None, None),
        P("grp", None),
        P(("grp", "shot"), None, None),
    )
    return jax.shard_map(
        shards,
        mesh=mesh,
        in_specs=placed,
        out_specs=(
            P(("grp", "blk"), None, None, None),
            P(("grp", "blk"), None, None, None),
            P(("grp", "shot"), None, "blk", None, None, None),
        ),
        check_vma=False,
    )
```

```python
import numpy as np
import jax
import jax.numpy as jnp
from jax import lax
from jax.experimental import pallas as pl
from jax.experimental.pallas import tpu as pltpu
from jax.sharding import PartitionSpec as P

STEPS = 2
YBLOCKS = 4
HALO = 4

A0 = -205.0 / 72.0
A = (8.0 / 5.0, -1.0 / 5.0, 8.0 / 315.0, -1.0 / 560.0)
C = (4.0 / 5.0, -1.0 / 5.0, 4.0 / 105.0, -1.0 / 280.0)
A_INT = (8064.0, -1008.0, 128.0, -9.0)
C_INT = (672.0, -168.0, 32.0, -3.0)
A_UNIT = 1.0 / 5040.0
C_UNIT = 1.0 / 840.0
TIME = 0.03
F32 = jnp.float32
BF16 = jnp.bfloat16
VMEM = pltpu.VMEM


def row_pairs(size):
    first, second = [], []
    for i in range(size):
        r = i // YBLOCKS
        partner = i + YBLOCKS if r % 2 == 0 else i - YBLOCKS
        if 0 <= partner < size:
            first.append((i, partner))
        partner = i + YBLOCKS if r % 2 == 1 else i - YBLOCKS
        if 0 <= partner < size:
            second.append((i, partner))
    return first, second


def column_pairs(size):
    first, second = [], []
    for i in range(size):
        c = i % YBLOCKS
        partner = c + 1 if c % 2 == 0 else c - 1
        if 0 <= partner < YBLOCKS:
            first.append((i, i - c + partner))
        partner = c + 1 if c % 2 == 1 else c - 1
        if 0 <= partner < YBLOCKS:
            second.append((i, i - c + partner))
    return first, second


def along_z(depth):
    lap = np.zeros((depth, depth), np.float32)
    slope = np.zeros((depth, depth), np.float32)
    for k in range(1, HALO + 1):
        i = np.arange(depth - k)
        lap[i + k, i] += A_INT[k - 1]
        lap[i, i + k] += A_INT[k - 1]
        slope[i + k, i] += C_INT[k - 1]
        slope[i, i + k] -= C_INT[k - 1]
    return np.concatenate([slope, lap], axis=1)


def along_y(height):
    out = []
    for parity in range(2):
        full = np.zeros((2, height, height + 2 * HALO), np.float32)
        for i in range(height):
            for k in range(1, HALO + 1):
                full[0, i, HALO + i + k] += C_INT[k - 1]
                full[0, i, HALO + i - k] -= C_INT[k - 1]
                full[1, i, HALO + i + k] += A_INT[k - 1]
                full[1, i, HALO + i - k] += A_INT[k - 1]
        full = full.reshape(2 * height, height + 2 * HALO)
        low, own, high = full[:, :HALO], full[:, HALO:-HALO], full[:, -HALO:]
        edge = np.concatenate([high, low] if parity == 0 else [low, high], axis=1)
        out.append(np.concatenate([own, own, edge, edge], axis=1))
    return np.stack(out)


def edge_rows(factor, height):
    rows = np.concatenate([np.arange(8), np.arange(height - 8, height)])
    return factor[:, np.concatenate([rows, height + rows]), 2 * height :]


def parts(value):
    lead = value.astype(BF16)
    return lead, (value - lead.astype(F32)).astype(BF16)


def dot(a, b):
    return jnp.dot(a, b, preferred_element_type=F32)


def z_product(block, factor):
    planes, height, depth = block.shape
    lead, trail = parts(block.reshape(planes * height, depth))
    out = dot(lead, factor) + dot(trail, factor)
    return out.reshape(planes, height, out.shape[1])


def edge_parts(first, second):
    edge = jnp.concatenate([first, second], axis=0)
    lead = edge.astype(BF16).astype(F32)
    return jnp.concatenate([lead, edge - lead], axis=0).astype(BF16)


def y_product(plane, first, second, factor):
    lead, trail = parts(plane)
    return dot(factor, jnp.concatenate([lead, trail, edge_parts(first, second)], axis=0))


def x_slope(own):
    out = []
    for i in range(len(own)):
        total = None
        for k in range(1, HALO + 1):
            if i + k < len(own) and i - k >= 0:
                term = C[k - 1] * (own[i + k] - own[i - k])
            elif i + k < len(own):
                term = C[k - 1] * own[i + k]
            elif i - k >= 0:
                term = -C[k - 1] * own[i - k]
            else:
                continue
            total = term if total is None else total + term
        out.append(total)
    return out


def x_laplace(own):
    out = []
    for i in range(len(own)):
        total = 3.0 * A0 * own[i]
        for k in range(1, HALO + 1):
            if i + k < len(own) and i - k >= 0:
                total = total + A[k - 1] * (own[i + k] + own[i - k])
            elif i + k < len(own):
                total = total + A[k - 1] * own[i + k]
            elif i - k >= 0:
                total = total + A[k - 1] * own[i - k]
        out.append(total)
    return out


def edge_terms(i, count, low, high):
    terms = []
    for k in range(1, HALO + 1):
        if i - k < 0 and low is not None:
            terms.append((k, -1.0, low[HALO + i - k]))
        if i + k >= count and high is not None:
            terms.append((k, 1.0, high[i + k - count]))
    return terms


def edge_slope(i, count, low, high):
    total = None
    for k, sign, value in edge_terms(i, count, low, high):
        term = (sign * C[k - 1]) * value
        total = term if total is None else total + term
    return total


def plus(value, *terms):
    for term in terms:
        value = value if term is None else value + term
    return value


def edge_laplace(i, count, low, high):
    total = None
    for k, _, value in edge_terms(i, count, low, high):
        term = A[k - 1] * value
        total = term if total is None else total + term
    return total


def depth_of_surface(topo_row, height):
    rows = lax.broadcasted_iota(jnp.int32, (height, height), 0)
    lanes = lax.broadcasted_iota(jnp.int32, (height, height), 1)
    picked = jnp.where(rows == lanes, topo_row.astype(F32), 0.0)
    return jnp.sum(picked, axis=1, keepdims=True).astype(jnp.int32)


def four(ref, rows):
    return None if ref is None else [ref[i, rows] for i in range(HALO)]


def two_and_two(first, second, rows):
    return [ref[HALO + i, rows] for ref in (first, second) for i in range(2)]


def row_parity():
    return lax.rem(lax.axis_index("blk") // YBLOCKS, 2)


def column_parity():
    return lax.rem(lax.rem(lax.axis_index("blk"), YBLOCKS), 2)


def copy_all(pairs, sem):
    copies = [pltpu.make_async_copy(a, b, sem.at[n]) for n, (a, b) in enumerate(pairs)]
    for c in copies:
        c.start()
    return copies


def first_kernel(adj, mod, buoy, topo_in, x1, x2, s0, cur_v, mod_v, topo, sem):
    width, height, depth = s0.shape
    parity = row_parity()
    first = pl.ds((1 - parity) * HALO, HALO)
    second = pl.ds(parity * HALO, HALO)
    copies = copy_all(
        [
            (topo_in, topo),
            (adj.at[0, 1, 0], cur_v),
            (mod.at[0], mod_v),
            (buoy.at[0, first], x1.at[0]),
            (buoy.at[0, second], x2.at[0]),
        ],
        sem,
    )
    lanes = lax.broadcasted_iota(jnp.int32, (height, depth), 1)
    copies[0].wait()
    masks = [lanes >= depth_of_surface(topo[0, i : i + 1, :], height) for i in range(width)]
    copies[1].wait()
    copies[2].wait()
    for i in range(width):
        s0[i] = jnp.where(masks[i], mod_v[i] * cur_v[i], 0.0)
    x1[1] = s0[first]
    x2[1] = s0[second]
    for c in copies[3:]:
        c.wait()


def edge_kernel(buoy, fwd, s0, y1, y2, low_v, high_v, sem):
    width, height, depth = s0.shape
    low, high = pl.ds(0, 8), pl.ds(height - 8, 8)
    copies = copy_all(
        [
            (buoy.at[0, :, low], low_v.at[0]),
            (buoy.at[0, :, high], high_v.at[0]),
            (fwd.at[0, pl.ds(1, 2), 0, :, low], low_v.at[pl.ds(1, 2)]),
            (fwd.at[0, pl.ds(1, 2), 0, :, high], high_v.at[pl.ds(1, 2)]),
        ],
        sem,
    )
    even = column_parity() == 0

    def pack(n, low, high):
        y1[n] = jnp.where(even, high, low)
        y2[n] = jnp.where(even, low, high)

    pack(1, s0[:, :HALO], s0[:, height - HALO :])
    for c in copies:
        c.wait()
    for n, m in ((0, 0), (2, 1), (3, 2)):
        pack(n, low_v[m, :, :HALO], high_v[m, :, 8 - HALO :])


def source_kernel(topo, rec, res, fwd, _, scale, source, x1, x2, s1, s2, sem):
    width, height, depth = scale.shape
    parity = row_parity()
    pairs = []
    for out, rest, at in ((x1, s1, (1 - parity) * HALO), (x2, s2, parity * HALO)):
        pairs += [
            (fwd.at[0, 1, 0, pl.ds(at, HALO)], out.at[pl.ds(0, HALO)]),
            (fwd.at[0, 2, 0, pl.ds(at, 2)], out.at[pl.ds(HALO, 2)]),
            (fwd.at[0, 2, 0, pl.ds(at + 2, 2)], rest.at[pl.ds(HALO, 2)]),
        ]
    copies = copy_all(pairs, sem)
    index = lax.axis_index("blk")
    anchor_x = index // YBLOCKS * width
    anchor_y = lax.rem(index, YBLOCKS) * height
    count = rec.shape[1]
    rx = rec[0:1, :] - anchor_x
    ry = rec[1:2, :] - anchor_y
    ids = lax.broadcasted_iota(jnp.int32, (STEPS * width, count), 0)
    values = jnp.concatenate(
        [jnp.broadcast_to(res[0, s : s + 1, :], (width, count)) for s in range(STEPS)], axis=0
    )
    hit_x = jnp.where(lax.rem(ids, width) == rx, values, 0.0)
    hit_y = (lax.broadcasted_iota(jnp.int32, (height, count), 0) == ry).astype(F32)
    plane = lax.dot_general(
        hit_y,
        hit_x,
        (((1,), (1,)), ((), ())),
        precision=lax.Precision.HIGHEST,
        preferred_element_type=F32,
    )
    lanes = lax.broadcasted_iota(jnp.int32, (height, depth), 1)
    for i in range(width):
        surface = depth_of_surface(topo[0, i : i + 1, :], height)
        live = lanes >= surface
        at = lanes == surface + 1
        scale[i] = jnp.where(live, TIME, 0.0)
        for s in range(STEPS):
            n = s * width + i
            source[s, i] = jnp.where(at, plane[:, n : n + 1], 0.0)
    for c in copies:
        c.wait()


def early_kernel(
    adj, buoy, s0, y1, y2, zf, yf, scale, source,
    rest, sx_own, sy, sz, gx_own, gy, gz, weight,
    zs, zb, ys, yb,
):
    width, height, depth = s0.shape
    factor_y = yf[column_parity()]
    zs[...] = z_product(s0[...], zf[...])
    zb[...] = z_product(buoy[0], zf[:, :depth])
    for i in range(width):
        ys[i] = y_product(s0[i], y1[1, i], y2[1, i], factor_y)
        yb[i] = y_product(buoy[0, i], y1[0, i], y2[0, i], factor_y[:height])
    for t in range(height // 8):
        rows = pl.ds(8 * t, 8)
        own = [s0[i, rows] for i in range(width)]
        slope = x_slope(own)
        laplace = x_laplace(own)
        for i in range(width):
            sx_own[i, rows] = slope[i]
            edge = ys[i, pl.ds(height + 8 * t, 8)] + zs[i, rows, depth:]
            laplace[i] = laplace[i] + A_UNIT * edge
        own = [buoy[0, i, rows] for i in range(width)]
        slope = x_slope(own)
        for i in range(width):
            w = scale[i, rows]
            gx_own[i, rows] = slope[i] * w
            g_y = (C_UNIT * w) * yb[i, rows]
            g_z = (C_UNIT * w) * zb[i, rows]
            s_y = C_UNIT * ys[i, rows]
            s_z = C_UNIT * zs[i, rows, :depth]
            b = own[i] * w
            weight[i, rows] = b
            gy[i, rows] = g_y
            gz[i, rows] = g_z
            sy[i, rows] = s_y
            sz[i, rows] = s_z
            moved = 2.0 * adj[0, 1, 0, i, rows] - adj[0, 0, 0, i, rows] + source[0, i, rows]
            moved = jnp.where(w > 0.0, moved, 0.0)
            rest[i, rows] = moved + b * laplace[i] + g_y * s_y + g_z * s_z


def finish_kernel(
    xa1, xa2, rest, sx_own, gx_own, weight, scale, mod, _f2, _x1, _x2,
    e0, s1, sx, gx, x1, x2, y1, y2, f2,
):
    width, height, depth = e0.shape

    def body(low_ref, high_ref, low_out, high_out):
        for t in range(height // 8):
            rows = pl.ds(8 * t, 8)
            low = [low_ref[1, i, rows] for i in range(HALO)]
            high = [high_ref[1, i, rows] for i in range(HALO)]
            low_b = [low_ref[0, i, rows] for i in range(HALO)]
            high_b = [high_ref[0, i, rows] for i in range(HALO)]
            for i in range(width):
                s_x = sx_own[i, rows] + edge_slope(i, width, low, high)
                g_x = gx_own[i, rows] + scale[i, rows] * edge_slope(i, width, low_b, high_b)
                earlier = (
                    rest[i, rows]
                    + weight[i, rows] * edge_laplace(i, width, low, high)
                    + g_x * s_x
                )
                scaled = mod[0, i, rows] * earlier
                sx[i, rows] = s_x
                gx[i, rows] = g_x
                e0[i, rows] = earlier
                s1[i, rows] = scaled
                if i < HALO:
                    low_out[i, rows] = scaled
                if i >= width - HALO:
                    high_out[i - (width - HALO), rows] = scaled

    @pl.when(row_parity() == 0)
    def _():
        body(xa2, xa1, x2, x1)

    @pl.when(row_parity() == 1)
    def _():
        body(xa1, xa2, x1, x2)

    even = column_parity() == 0
    y1[...] = jnp.where(even, s1[:, height - HALO :], s1[:, :HALO])
    y2[...] = jnp.where(even, s1[:, :8], s1[:, height - 8 :])


def middle_kernel(
    adj, e0, s1, sx0, sy0, sz0, gy, gz, weight, scale, source, fwd, xf, yf1, yf2, zf, yf,
    rest, sx_own, image, fx, fy, image_mod, states,
    zs, ys, z1, z2, ya, image_v, sem,
):
    width, height, depth = e0.shape
    first = pltpu.make_async_copy(e0, states.at[0, 0, 0], sem.at[0])
    first.start()
    for i in range(width):
        f0, f1, f2, f3 = (fwd[0, n, 0, i] for n in range(4))
        image_v[i] = adj[0, 1, 0, i] * (f0 - 2.0 * f1 + f2) + e0[i] * (f1 - 2.0 * f2 + f3)
    second = pltpu.make_async_copy(image_v, image_mod.at[0], sem.at[1])
    second.start()
    factor_y = yf[column_parity()]
    factor_own = factor_y[:, : 2 * height]
    zs[...] = z_product(s1[...], zf[...])
    z1[...] = z_product(fwd[0, 1, 0], zf[:, :depth])
    z2[...] = z_product(fwd[0, 2, 0], zf[:, :depth])
    for i in range(width):
        ys[i] = dot(factor_own, jnp.concatenate(parts(s1[i]), axis=0))
        ya[i] = y_product(fwd[0, 1, 0, i], yf1[2, i], yf2[2, i], factor_y[:height])
        fy[i] = y_product(fwd[0, 2, 0, i], yf1[3, i], yf2[3, i], factor_y[:height])

    def body(low_ref, high_ref):
        for t in range(height // 8):
            rows = pl.ds(8 * t, 8)
            own = [s1[i, rows] for i in range(width)]
            slope = x_slope(own)
            laplace = x_laplace(own)
            own1 = [fwd[0, 1, 0, i, rows] for i in range(width)]
            own2 = [fwd[0, 2, 0, i, rows] for i in range(width)]
            slope1 = x_slope(own1)
            slope2 = x_slope(own2)
            low1, high1 = four(low_ref, rows), four(high_ref, rows)
            for i in range(width):
                now, before = adj[0, 1, 0, i, rows], e0[i, rows]
                s_y = C_UNIT * ys[i, rows]
                s_z = C_UNIT * zs[i, rows, :depth]
                edge = ys[i, pl.ds(height + 8 * t, 8)] + zs[i, rows, depth:]
                lap = laplace[i] + A_UNIT * edge
                moved = 2.0 * before - now + source[1, i, rows]
                moved = jnp.where(scale[i, rows] > 0.0, moved, 0.0)
                rest[i, rows] = (
                    moved + weight[i, rows] * lap + gy[i, rows] * s_y + gz[i, rows] * s_z
                )
                sx_own[i, rows] = slope[i]
                f1x = plus(slope1[i], edge_slope(i, width, low1, high1))
                fx[i, rows] = slope2[i]
                image[i, rows] = (
                    f1x * sx0[i, rows]
                    + C_UNIT
                    * (
                        ya[i, rows] * sy0[i, rows]
                        + z1[i, rows] * sz0[i, rows]
                        + fy[i, rows] * s_y
                        + z2[i, rows] * s_z
                    )
                )

    @pl.when(row_parity() == 0)
    def _():
        body(None, xf)

    @pl.when(row_parity() == 1)
    def _():
        body(xf, None)

    first.wait()
    second.wait()


def last_kernel(
    xs1, xs2, ys1, ys2, rest, sx_own, image, fx, fy, gx, gy, weight, ye, sx0, xf1, xf2, states_in,
    image_out, states_out,
    image_v, e1_v, sem,
):
    width, height, depth = rest.shape
    tiles = height // 8
    factor = ye[column_parity()]

    def leave(t):
        rows = pl.ds(8 * t, 8)
        return (
            pltpu.make_async_copy(e1_v.at[:, rows], states_out.at[0, 1, 0, :, rows], sem.at[t]),
            pltpu.make_async_copy(image_v.at[:, rows], image_out.at[0, :, rows], sem.at[tiles + t]),
        )

    even = column_parity() == 0

    def edge_of(i):
        second = jnp.where(even, ys2[i, 8 - HALO :], ys2[i, :HALO])
        return dot(factor, edge_parts(ys1[i], second))

    def body(low_ref, high_ref, low_fields, high_fields, low_one, high_one):
        edges = [edge_of(i) for i in range(width)]
        for t in list(range(1, tiles - 1)) + [0, tiles - 1]:
            rows = pl.ds(8 * t, 8)
            low = [low_ref[i, rows] for i in range(HALO)]
            high = [high_ref[i, rows] for i in range(HALO)]
            low1, high1 = four(low_one, rows), four(high_one, rows)
            low2 = two_and_two(low_fields, low_ref, rows)
            high2 = two_and_two(high_fields, high_ref, rows)
            for i in range(width):
                s_x = sx_own[i, rows] + edge_slope(i, width, low, high)
                lap = edge_laplace(i, width, low, high)
                add = gx[i, rows] * s_x
                f_x = plus(fx[i, rows], edge_slope(i, width, low2, high2))
                shown = image[i, rows] + f_x * s_x
                f_x = edge_slope(i, width, low1, high1)
                if f_x is not None:
                    shown = shown + f_x * sx0[i, rows]
                if t == 0 or t == tiles - 1:
                    n = 0 if t == 0 else 8
                    s_y = C_UNIT * edges[i][n : n + 8]
                    lap = lap + A_UNIT * edges[i][16 + n : 24 + n]
                    add = add + gy[i, rows] * s_y
                    shown = shown + C_UNIT * (fy[i, rows] * s_y)
                e1_v[i, rows] = rest[i, rows] + weight[i, rows] * lap + add
                image_v[i, rows] = shown
            for c in leave(t):
                c.start()

    @pl.when(row_parity() == 0)
    def _():
        body(xs2, xs1, xf2, xf1, xf2, None)

    @pl.when(row_parity() == 1)
    def _():
        body(xs1, xs2, xf1, xf2, None, xf2)

    for t in range(tiles):
        for c in leave(t):
            c.wait()


def call(kernel, name, inputs, outputs, scratch=(), us=1.0, aliases=None):
    arrays, in_specs = [], []
    for array, near in inputs:
        place = VMEM if near else pltpu.HBM
        arrays.append(pltpu.with_memory_space_constraint(array, place))
        in_specs.append(pl.BlockSpec(memory_space=place))
    shapes, out_specs = [], []
    for shape, near in outputs:
        place = VMEM if near else pltpu.HBM
        shapes.append(place(shape, F32))
        out_specs.append(pl.BlockSpec(memory_space=place))
    return pl.pallas_call(
        kernel,
        name=name,
        in_specs=in_specs,
        out_specs=out_specs,
        out_shape=shapes,
        scratch_shapes=list(scratch),
        input_output_aliases=aliases or {},
        compiler_params=pltpu.CompilerParams(vmem_limit_bytes=16 * 1024 * 1024),
        cost_estimate=pl.CostEstimate(
            flops=0, bytes_accessed=int(us * 3.0e6), transcendentals=0
        ),
    )(*arrays)


def shards(adjoint_in, forward, modulus, buoyancy, topography, receivers, residuals):
    width, height, depth = modulus.shape[1:]
    block = (width, height, depth)
    size = lax.axis_size("blk")
    rows1, rows2 = row_pairs(size)
    cols1, cols2 = column_pairs(size)
    zf = jnp.asarray(along_z(depth), BF16)
    yf = jnp.asarray(along_y(height), BF16)
    ye = jnp.asarray(edge_rows(along_y(height), height), BF16)
    dma = pltpu.SemaphoreType.DMA

    def swap(value, pairs):
        return lax.ppermute(value, "blk", pairs)

    ahead = (2, HALO, height, depth)
    six = (HALO + 2, height, depth)
    edge = (4, width, HALO, depth)
    xa1, xa2, s0 = call(
        first_kernel,
        "scaled_and_planes",
        [(adjoint_in, False), (modulus, False), (buoyancy, False), (topography, False)],
        [(ahead, True)] * 2 + [(block, True)],
        [VMEM(block, F32), VMEM(block, F32), VMEM(topography.shape, jnp.int32), dma((5,))],
    )
    xa1, xa2 = swap(xa1, rows1), swap(xa2, rows2)
    ya1, ya2 = call(
        edge_kernel,
        "edges",
        [(buoyancy, False), (forward, False), (s0, True)],
        [(edge, True)] * 2,
        [VMEM((3, width, 8, depth), F32), VMEM((3, width, 8, depth), F32), dma((4,))],
    )
    ya1, ya2 = swap(ya1, cols1), swap(ya2, cols2)
    z_out = (width, height, 2 * depth)
    y_out = (width, 2 * height, depth)
    scale, source, xf1, xf2, xs1, xs2 = call(
        source_kernel,
        "sources_and_planes",
        [(topography, True), (receivers.T, True), (residuals, True), (forward, False), (ya1, True)],
        [(block, True), ((STEPS,) + block, True)] + [(six, True)] * 4,
        [dma((6,))],
    )
    xf1 = swap(xf1, rows1)
    rest, sx_own, sy, sz, gx_own, gy, gz, weight = call(
        early_kernel,
        "step0_own",
        [(adjoint_in, True), (buoyancy, True), (s0, True), (ya1, True), (ya2, True), (zf, True), (yf, True),
         (scale, True), (source, True)],
        [(block, True)] * 8,
        [VMEM(z_out, F32), VMEM(block, F32), VMEM(y_out, F32), VMEM(block, F32)],
        us=4.0,
    )
    side = (width, HALO, depth)
    rows8 = (width, 8, depth)
    e0, s1, sx, gx, xs1, xs2, ys1, ys2, xf2 = call(
        finish_kernel,
        "step0_planes",
        [(xa1, True), (xa2, True), (rest, True), (sx_own, True), (gx_own, True), (weight, True), (scale, True),
         (modulus, True), (xf2, True), (xs1, True), (xs2, True)],
        [(block, True)] * 4 + [(six, True)] * 2 + [(side, True), (rows8, True), (six, True)],
        aliases={8: 8, 9: 4, 10: 5},
    )
    xs1, xf2, xs2 = swap(xs1, rows1), swap(xf2, rows2), swap(xs2, rows2)
    ys1, ys2 = swap(ys1, cols1), swap(ys2, cols2)
    rest, sx_own, image, fx, fy, image_mod, states = call(
        middle_kernel,
        "images_and_step1_own",
        [(adjoint_in, True), (e0, True), (s1, True), (sx, True), (sy, True), (sz, True), (gy, True), (gz, True),
         (weight, True), (scale, True), (source, True), (forward, True), (xf1, True), (ya1, True),
         (ya2, True), (zf, True), (yf, True)],
        [(block, True)] * 5 + [((1,) + block, False), ((1, STEPS, 1) + block, False)],
        [VMEM(z_out, F32), VMEM(y_out, F32)] + [VMEM(block, F32)] * 4 + [dma((2,))],
        us=20.0,
    )
    image_buo, states = call(
        last_kernel,
        "step1_planes",
        [(xs1, True), (xs2, True), (ys1, True), (ys2, True), (rest, True), (sx_own, True), (image, True), (fx, True),
         (fy, True), (gx, True), (gy, True), (weight, True), (ye, True), (sx, True), (xf1, True), (xf2, True), (states, False)],
        [((1,) + block, False), ((1, STEPS, 1) + block, False)],
        [VMEM(block, F32), VMEM(block, F32), dma((2 * (height // 8),))],
        aliases={16: 1},
    )
    if lax.axis_size("shot") > 1:
        image_mod, image_buo = lax.psum((image_mod, image_buo), "shot")
    return image_mod, image_buo, states


def solution(mesh):
    placed = (
        P(("grp", "shot"), None, "blk", None, None, None),
        P(("grp", "shot"), None, "blk", None, None, None),
        P(("grp", "blk"), None, None, None),
        P(("grp", "blk"), None, None, None),
        P(("grp", "blk"), None, None),
        P("grp", None),
        P(("grp", "shot"), None, None),
    )
    return jax.shard_map(
        shards,
        mesh=mesh,
        in_specs=placed,
        out_specs=(
            P(("grp", "blk"), None, None, None),
            P(("grp", "blk"), None, None, None),
            P(("grp", "shot"), None, "blk", None, None, None),
        ),
        check_vma=False,
    )
```

```python
import numpy as np
import jax
import jax.numpy as jnp
from jax import lax
from jax.experimental import pallas as pl
from jax.experimental.pallas import tpu as pltpu
from jax.sharding import PartitionSpec as P

STEPS = 2
YBLOCKS = 4
HALO = 4

A0 = -205.0 / 72.0
A = (8.0 / 5.0, -1.0 / 5.0, 8.0 / 315.0, -1.0 / 560.0)
C = (4.0 / 5.0, -1.0 / 5.0, 4.0 / 105.0, -1.0 / 280.0)
A_INT = (8064.0, -1008.0, 128.0, -9.0)
C_INT = (672.0, -168.0, 32.0, -3.0)
A_UNIT = 1.0 / 5040.0
C_UNIT = 1.0 / 840.0
TIME = 0.03
F32 = jnp.float32
BF16 = jnp.bfloat16
VMEM = pltpu.VMEM


def row_pairs(size):
    first, second = [], []
    for i in range(size):
        r = i // YBLOCKS
        partner = i + YBLOCKS if r % 2 == 0 else i - YBLOCKS
        if 0 <= partner < size:
            first.append((i, partner))
        partner = i + YBLOCKS if r % 2 == 1 else i - YBLOCKS
        if 0 <= partner < size:
            second.append((i, partner))
    return first, second


def column_pairs(size):
    first, second = [], []
    for i in range(size):
        c = i % YBLOCKS
        partner = c + 1 if c % 2 == 0 else c - 1
        if 0 <= partner < YBLOCKS:
            first.append((i, i - c + partner))
        partner = c + 1 if c % 2 == 1 else c - 1
        if 0 <= partner < YBLOCKS:
            second.append((i, i - c + partner))
    return first, second


def along_z(depth):
    lap = np.zeros((depth, depth), np.float32)
    slope = np.zeros((depth, depth), np.float32)
    for k in range(1, HALO + 1):
        i = np.arange(depth - k)
        lap[i + k, i] += A_INT[k - 1]
        lap[i, i + k] += A_INT[k - 1]
        slope[i + k, i] += C_INT[k - 1]
        slope[i, i + k] -= C_INT[k - 1]
    return np.concatenate([slope, lap], axis=1)


def along_y(height):
    out = []
    for parity in range(2):
        full = np.zeros((2, height, height + 2 * HALO), np.float32)
        for i in range(height):
            for k in range(1, HALO + 1):
                full[0, i, HALO + i + k] += C_INT[k - 1]
                full[0, i, HALO + i - k] -= C_INT[k - 1]
                full[1, i, HALO + i + k] += A_INT[k - 1]
                full[1, i, HALO + i - k] += A_INT[k - 1]
        full = full.reshape(2 * height, height + 2 * HALO)
        low, own, high = full[:, :HALO], full[:, HALO:-HALO], full[:, -HALO:]
        edge = np.concatenate([high, low] if parity == 0 else [low, high], axis=1)
        out.append(np.concatenate([own, own, edge, edge], axis=1))
    return np.stack(out)


def edge_rows(factor, height):
    rows = np.concatenate([np.arange(8), np.arange(height - 8, height)])
    return factor[:, np.concatenate([rows, height + rows]), 2 * height :]


def parts(value):
    lead = value.astype(BF16)
    return lead, (value - lead.astype(F32)).astype(BF16)


def dot(a, b):
    return jnp.dot(a, b, preferred_element_type=F32)


def z_product(block, factor):
    planes, height, depth = block.shape
    lead, trail = parts(block.reshape(planes * height, depth))
    out = dot(lead, factor) + dot(trail, factor)
    return out.reshape(planes, height, out.shape[1])


def edge_parts(first, second):
    edge = jnp.concatenate([first, second], axis=0)
    lead = edge.astype(BF16).astype(F32)
    return jnp.concatenate([lead, edge - lead], axis=0).astype(BF16)


def y_product(plane, first, second, factor):
    lead, trail = parts(plane)
    return dot(factor, jnp.concatenate([lead, trail, edge_parts(first, second)], axis=0))


def x_slope(own):
    out = []
    for i in range(len(own)):
        total = None
        for k in range(1, HALO + 1):
            if i + k < len(own) and i - k >= 0:
                term = C[k - 1] * (own[i + k] - own[i - k])
            elif i + k < len(own):
                term = C[k - 1] * own[i + k]
            elif i - k >= 0:
                term = -C[k - 1] * own[i - k]
            else:
                continue
            total = term if total is None else total + term
        out.append(total)
    return out


def x_laplace(own):
    out = []
    for i in range(len(own)):
        total = 3.0 * A0 * own[i]
        for k in range(1, HALO + 1):
            if i + k < len(own) and i - k >= 0:
                total = total + A[k - 1] * (own[i + k] + own[i - k])
            elif i + k < len(own):
                total = total + A[k - 1] * own[i + k]
            elif i - k >= 0:
                total = total + A[k - 1] * own[i - k]
        out.append(total)
    return out


def edge_terms(i, count, low, high):
    terms = []
    for k in range(1, HALO + 1):
        if i - k < 0 and low is not None:
            terms.append((k, -1.0, low[HALO + i - k]))
        if i + k >= count and high is not None:
            terms.append((k, 1.0, high[i + k - count]))
    return terms


def edge_slope(i, count, low, high):
    total = None
    for k, sign, value in edge_terms(i, count, low, high):
        term = (sign * C[k - 1]) * value
        total = term if total is None else total + term
    return total


def plus(value, *terms):
    for term in terms:
        value = value if term is None else value + term
    return value


def edge_laplace(i, count, low, high):
    total = None
    for k, _, value in edge_terms(i, count, low, high):
        term = A[k - 1] * value
        total = term if total is None else total + term
    return total


def depth_of_surface(topo_row, height):
    rows = lax.broadcasted_iota(jnp.int32, (height, height), 0)
    lanes = lax.broadcasted_iota(jnp.int32, (height, height), 1)
    picked = jnp.where(rows == lanes, topo_row.astype(F32), 0.0)
    return jnp.sum(picked, axis=1, keepdims=True).astype(jnp.int32)


def four(ref, rows):
    return None if ref is None else [ref[i, rows] for i in range(HALO)]


def two_and_two(first, second, rows):
    return [ref[HALO + i, rows] for ref in (first, second) for i in range(2)]


def row_parity():
    return lax.rem(lax.axis_index("blk") // YBLOCKS, 2)


def column_parity():
    return lax.rem(lax.rem(lax.axis_index("blk"), YBLOCKS), 2)


def copy_all(pairs, sem):
    copies = [pltpu.make_async_copy(a, b, sem.at[n]) for n, (a, b) in enumerate(pairs)]
    for c in copies:
        c.start()
    return copies


def first_kernel(adj, mod, buoy, topo_in, x1, x2, s0, cur_v, mod_v, topo, sem):
    width, height, depth = s0.shape
    parity = row_parity()
    first = pl.ds((1 - parity) * HALO, HALO)
    second = pl.ds(parity * HALO, HALO)
    copies = copy_all(
        [
            (topo_in, topo),
            (adj.at[0, 1, 0], cur_v),
            (mod.at[0], mod_v),
            (buoy.at[0, first], x1.at[0]),
            (buoy.at[0, second], x2.at[0]),
        ],
        sem,
    )
    lanes = lax.broadcasted_iota(jnp.int32, (height, depth), 1)
    copies[0].wait()
    masks = [lanes >= depth_of_surface(topo[0, i : i + 1, :], height) for i in range(width)]
    copies[1].wait()
    copies[2].wait()
    for i in range(width):
        s0[i] = jnp.where(masks[i], mod_v[i] * cur_v[i], 0.0)
    x1[1] = s0[first]
    x2[1] = s0[second]
    for c in copies[3:]:
        c.wait()


def edge_kernel(buoy, fwd, s0, y1, y2, low_v, high_v, sem):
    width, height, depth = s0.shape
    low, high = pl.ds(0, 8), pl.ds(height - 8, 8)
    copies = copy_all(
        [
            (buoy.at[0, :, low], low_v.at[0]),
            (buoy.at[0, :, high], high_v.at[0]),
            (fwd.at[0, pl.ds(1, 2), 0, :, low], low_v.at[pl.ds(1, 2)]),
            (fwd.at[0, pl.ds(1, 2), 0, :, high], high_v.at[pl.ds(1, 2)]),
        ],
        sem,
    )
    even = column_parity() == 0

    def pack(n, low, high):
        y1[n] = jnp.where(even, high, low)
        y2[n] = jnp.where(even, low, high)

    pack(1, s0[:, :HALO], s0[:, height - HALO :])
    for c in copies:
        c.wait()
    for n, m in ((0, 0), (2, 1), (3, 2)):
        pack(n, low_v[m, :, :HALO], high_v[m, :, 8 - HALO :])


def source_kernel(topo, rec, res, fwd, _, scale, source, x1, x2, s1, s2, sem):
    width, height, depth = scale.shape
    parity = row_parity()
    pairs = []
    for out, rest, at in ((x1, s1, (1 - parity) * HALO), (x2, s2, parity * HALO)):
        pairs += [
            (fwd.at[0, 1, 0, pl.ds(at, HALO)], out.at[pl.ds(0, HALO)]),
            (fwd.at[0, 2, 0, pl.ds(at, 2)], out.at[pl.ds(HALO, 2)]),
            (fwd.at[0, 2, 0, pl.ds(at + 2, 2)], rest.at[pl.ds(HALO, 2)]),
        ]
    copies = copy_all(pairs, sem)
    index = lax.axis_index("blk")
    anchor_x = index // YBLOCKS * width
    anchor_y = lax.rem(index, YBLOCKS) * height
    count = rec.shape[1]
    rx = rec[0:1, :] - anchor_x
    ry = rec[1:2, :] - anchor_y
    ids = lax.broadcasted_iota(jnp.int32, (STEPS * width, count), 0)
    values = jnp.concatenate(
        [jnp.broadcast_to(res[0, s : s + 1, :], (width, count)) for s in range(STEPS)], axis=0
    )
    hit_x = jnp.where(lax.rem(ids, width) == rx, values, 0.0)
    hit_y = (lax.broadcasted_iota(jnp.int32, (height, count), 0) == ry).astype(F32)
    plane = lax.dot_general(
        hit_y,
        hit_x,
        (((1,), (1,)), ((), ())),
        precision=lax.Precision.HIGHEST,
        preferred_element_type=F32,
    )
    lanes = lax.broadcasted_iota(jnp.int32, (height, depth), 1)
    for i in range(width):
        surface = depth_of_surface(topo[0, i : i + 1, :], height)
        live = lanes >= surface
        at = lanes == surface + 1
        scale[i] = jnp.where(live, TIME, 0.0)
        for s in range(STEPS):
            n = s * width + i
            source[s, i] = jnp.where(at, plane[:, n : n + 1], 0.0)
    for c in copies:
        c.wait()


def early_kernel(
    adj, buoy, s0, y1, y2, zf, yf, scale, source,
    rest, sx_own, sy, sz, gx_own, gy, gz, weight,
    zs, zb, ys, yb,
):
    width, height, depth = s0.shape
    factor_y = yf[column_parity()]
    zs[...] = z_product(s0[...], zf[...])
    zb[...] = z_product(buoy[0], zf[:, :depth])
    for i in range(width):
        ys[i] = y_product(s0[i], y1[1, i], y2[1, i], factor_y)
        yb[i] = y_product(buoy[0, i], y1[0, i], y2[0, i], factor_y[:height])
    for t in range(height // 8):
        rows = pl.ds(8 * t, 8)
        own = [s0[i, rows] for i in range(width)]
        slope = x_slope(own)
        laplace = x_laplace(own)
        for i in range(width):
            sx_own[i, rows] = slope[i]
            edge = ys[i, pl.ds(height + 8 * t, 8)] + zs[i, rows, depth:]
            laplace[i] = laplace[i] + A_UNIT * edge
        own = [buoy[0, i, rows] for i in range(width)]
        slope = x_slope(own)
        for i in range(width):
            w = scale[i, rows]
            gx_own[i, rows] = slope[i] * w
            g_y = (C_UNIT * w) * yb[i, rows]
            g_z = (C_UNIT * w) * zb[i, rows]
            s_y = C_UNIT * ys[i, rows]
            s_z = C_UNIT * zs[i, rows, :depth]
            b = own[i] * w
            weight[i, rows] = b
            gy[i, rows] = g_y
            gz[i, rows] = g_z
            sy[i, rows] = s_y
            sz[i, rows] = s_z
            moved = 2.0 * adj[0, 1, 0, i, rows] - adj[0, 0, 0, i, rows] + source[0, i, rows]
            moved = jnp.where(w > 0.0, moved, 0.0)
            rest[i, rows] = moved + b * laplace[i] + g_y * s_y + g_z * s_z


def finish_kernel(
    xa1, xa2, rest, sx_own, gx_own, weight, scale, mod, _f2, _x1, _x2,
    e0, s1, sx, gx, x1, x2, y1, y2, f2,
):
    width, height, depth = e0.shape

    def body(low_ref, high_ref, low_out, high_out):
        for t in range(height // 8):
            rows = pl.ds(8 * t, 8)
            low = [low_ref[1, i, rows] for i in range(HALO)]
            high = [high_ref[1, i, rows] for i in range(HALO)]
            low_b = [low_ref[0, i, rows] for i in range(HALO)]
            high_b = [high_ref[0, i, rows] for i in range(HALO)]
            for i in range(width):
                s_x = sx_own[i, rows] + edge_slope(i, width, low, high)
                g_x = gx_own[i, rows] + scale[i, rows] * edge_slope(i, width, low_b, high_b)
                earlier = (
                    rest[i, rows]
                    + weight[i, rows] * edge_laplace(i, width, low, high)
                    + g_x * s_x
                )
                scaled = mod[0, i, rows] * earlier
                sx[i, rows] = s_x
                gx[i, rows] = g_x
                e0[i, rows] = earlier
                s1[i, rows] = scaled
                if i < HALO:
                    low_out[i, rows] = scaled
                if i >= width - HALO:
                    high_out[i - (width - HALO), rows] = scaled

    @pl.when(row_parity() == 0)
    def _():
        body(xa2, xa1, x2, x1)

    @pl.when(row_parity() == 1)
    def _():
        body(xa1, xa2, x1, x2)

    even = column_parity() == 0
    y1[...] = jnp.where(even, s1[:, height - HALO :], s1[:, :HALO])
    y2[...] = jnp.where(even, s1[:, :8], s1[:, height - 8 :])


def middle_kernel(
    adj, e0, s1, sx0, sy0, sz0, gy, gz, weight, scale, source, fwd, xf, yf1, yf2, zf, yf,
    rest, sx_own, image, fx, fy, image_mod, states,
    zs, ys, z1, z2, ya, image_v, sem,
):
    width, height, depth = e0.shape
    first = pltpu.make_async_copy(e0, states.at[0, 0, 0], sem.at[0])
    first.start()
    for i in range(width):
        f0, f1, f2, f3 = (fwd[0, n, 0, i] for n in range(4))
        image_v[i] = adj[0, 1, 0, i] * (f0 - 2.0 * f1 + f2) + e0[i] * (f1 - 2.0 * f2 + f3)
    second = pltpu.make_async_copy(image_v, image_mod.at[0], sem.at[1])
    second.start()
    factor_y = yf[column_parity()]
    factor_own = factor_y[:, : 2 * height]
    zs[...] = z_product(s1[...], zf[...])
    z1[...] = z_product(fwd[0, 1, 0], zf[:, :depth])
    z2[...] = z_product(fwd[0, 2, 0], zf[:, :depth])
    for i in range(width):
        ys[i] = dot(factor_own, jnp.concatenate(parts(s1[i]), axis=0))
        ya[i] = y_product(fwd[0, 1, 0, i], yf1[2, i], yf2[2, i], factor_y[:height])
        fy[i] = y_product(fwd[0, 2, 0, i], yf1[3, i], yf2[3, i], factor_y[:height])

    def body(low_ref, high_ref):
        for t in range(height // 8):
            rows = pl.ds(8 * t, 8)
            own = [s1[i, rows] for i in range(width)]
            slope = x_slope(own)
            laplace = x_laplace(own)
            own1 = [fwd[0, 1, 0, i, rows] for i in range(width)]
            own2 = [fwd[0, 2, 0, i, rows] for i in range(width)]
            slope1 = x_slope(own1)
            slope2 = x_slope(own2)
            low1, high1 = four(low_ref, rows), four(high_ref, rows)
            for i in range(width):
                now, before = adj[0, 1, 0, i, rows], e0[i, rows]
                s_y = C_UNIT * ys[i, rows]
                s_z = C_UNIT * zs[i, rows, :depth]
                edge = ys[i, pl.ds(height + 8 * t, 8)] + zs[i, rows, depth:]
                lap = laplace[i] + A_UNIT * edge
                moved = 2.0 * before - now + source[1, i, rows]
                moved = jnp.where(scale[i, rows] > 0.0, moved, 0.0)
                rest[i, rows] = (
                    moved + weight[i, rows] * lap + gy[i, rows] * s_y + gz[i, rows] * s_z
                )
                sx_own[i, rows] = slope[i]
                f1x = plus(slope1[i], edge_slope(i, width, low1, high1))
                fx[i, rows] = slope2[i]
                image[i, rows] = (
                    f1x * sx0[i, rows]
                    + C_UNIT
                    * (
                        ya[i, rows] * sy0[i, rows]
                        + z1[i, rows] * sz0[i, rows]
                        + fy[i, rows] * s_y
                        + z2[i, rows] * s_z
                    )
                )

    @pl.when(row_parity() == 0)
    def _():
        body(None, xf)

    @pl.when(row_parity() == 1)
    def _():
        body(xf, None)

    first.wait()
    second.wait()


def column_kernel(ys1, ys2, weight, gy, fy, ye, rest_in, image_in, rest, image):
    width, height, depth = weight.shape
    factor = ye[column_parity()]
    even = column_parity() == 0
    for i in range(width):
        second = jnp.where(even, ys2[i, 8 - HALO :], ys2[i, :HALO])
        edge = dot(factor, edge_parts(ys1[i], second))
        for n, start in ((0, 0), (8, height - 8)):
            rows = pl.ds(start, 8)
            s_y = C_UNIT * edge[n : n + 8]
            lap = A_UNIT * edge[16 + n : 24 + n]
            rest[i, rows] = rest_in[i, rows] + weight[i, rows] * lap + gy[i, rows] * s_y
            image[i, rows] = image_in[i, rows] + C_UNIT * (fy[i, rows] * s_y)


def last_kernel(
    xs1, xs2, rest, sx_own, image, fx, gx, weight, sx0, xf1, xf2, states_in,
    image_out, states_out,
    image_v, e1_v, sem,
):
    width, height, depth = rest.shape
    tiles = height // 8

    def leave(t):
        rows = pl.ds(8 * t, 8)
        return (
            pltpu.make_async_copy(e1_v.at[:, rows], states_out.at[0, 1, 0, :, rows], sem.at[t]),
            pltpu.make_async_copy(image_v.at[:, rows], image_out.at[0, :, rows], sem.at[tiles + t]),
        )

    def body(low_ref, high_ref, low_fields, high_fields, low_one, high_one):
        for t in range(tiles):
            rows = pl.ds(8 * t, 8)
            low = [low_ref[i, rows] for i in range(HALO)]
            high = [high_ref[i, rows] for i in range(HALO)]
            low1, high1 = four(low_one, rows), four(high_one, rows)
            low2 = two_and_two(low_fields, low_ref, rows)
            high2 = two_and_two(high_fields, high_ref, rows)
            for i in range(width):
                s_x = sx_own[i, rows] + edge_slope(i, width, low, high)
                lap = edge_laplace(i, width, low, high)
                add = gx[i, rows] * s_x
                f_x = plus(fx[i, rows], edge_slope(i, width, low2, high2))
                shown = image[i, rows] + f_x * s_x
                f_x = edge_slope(i, width, low1, high1)
                if f_x is not None:
                    shown = shown + f_x * sx0[i, rows]
                e1_v[i, rows] = rest[i, rows] + weight[i, rows] * lap + add
                image_v[i, rows] = shown
            for c in leave(t):
                c.start()

    @pl.when(row_parity() == 0)
    def _():
        body(xs2, xs1, xf2, xf1, xf2, None)

    @pl.when(row_parity() == 1)
    def _():
        body(xs1, xs2, xf1, xf2, None, xf2)

    for t in range(tiles):
        for c in leave(t):
            c.wait()


def call(kernel, name, inputs, outputs, scratch=(), us=1.0, aliases=None):
    arrays, in_specs = [], []
    for array, near in inputs:
        place = VMEM if near else pltpu.HBM
        arrays.append(pltpu.with_memory_space_constraint(array, place))
        in_specs.append(pl.BlockSpec(memory_space=place))
    shapes, out_specs = [], []
    for shape, near in outputs:
        place = VMEM if near else pltpu.HBM
        shapes.append(place(shape, F32))
        out_specs.append(pl.BlockSpec(memory_space=place))
    return pl.pallas_call(
        kernel,
        name=name,
        in_specs=in_specs,
        out_specs=out_specs,
        out_shape=shapes,
        scratch_shapes=list(scratch),
        input_output_aliases=aliases or {},
        compiler_params=pltpu.CompilerParams(vmem_limit_bytes=16 * 1024 * 1024),
        cost_estimate=pl.CostEstimate(
            flops=0, bytes_accessed=int(us * 3.0e6), transcendentals=0
        ),
    )(*arrays)


def shards(adjoint_in, forward, modulus, buoyancy, topography, receivers, residuals):
    width, height, depth = modulus.shape[1:]
    block = (width, height, depth)
    size = lax.axis_size("blk")
    rows1, rows2 = row_pairs(size)
    cols1, cols2 = column_pairs(size)
    zf = jnp.asarray(along_z(depth), BF16)
    yf = jnp.asarray(along_y(height), BF16)
    ye = jnp.asarray(edge_rows(along_y(height), height), BF16)
    dma = pltpu.SemaphoreType.DMA

    def swap(value, pairs):
        return lax.ppermute(value, "blk", pairs)

    ahead = (2, HALO, height, depth)
    six = (HALO + 2, height, depth)
    edge = (4, width, HALO, depth)
    xa1, xa2, s0 = call(
        first_kernel,
        "scaled_and_planes",
        [(adjoint_in, False), (modulus, False), (buoyancy, False), (topography, False)],
        [(ahead, True)] * 2 + [(block, True)],
        [VMEM(block, F32), VMEM(block, F32), VMEM(topography.shape, jnp.int32), dma((5,))],
    )
    xa1, xa2 = swap(xa1, rows1), swap(xa2, rows2)
    ya1, ya2 = call(
        edge_kernel,
        "edges",
        [(buoyancy, False), (forward, False), (s0, True)],
        [(edge, True)] * 2,
        [VMEM((3, width, 8, depth), F32), VMEM((3, width, 8, depth), F32), dma((4,))],
    )
    ya1, ya2 = swap(ya1, cols1), swap(ya2, cols2)
    z_out = (width, height, 2 * depth)
    y_out = (width, 2 * height, depth)
    scale, source, xf1, xf2, xs1, xs2 = call(
        source_kernel,
        "sources_and_planes",
        [(topography, True), (receivers.T, True), (residuals, True), (forward, False), (ya1, True)],
        [(block, True), ((STEPS,) + block, True)] + [(six, True)] * 4,
        [dma((6,))],
    )
    xf1 = swap(xf1, rows1)
    rest, sx_own, sy, sz, gx_own, gy, gz, weight = call(
        early_kernel,
        "step0_own",
        [(adjoint_in, True), (buoyancy, True), (s0, True), (ya1, True), (ya2, True), (zf, True), (yf, True),
         (scale, True), (source, True)],
        [(block, True)] * 8,
        [VMEM(z_out, F32), VMEM(block, F32), VMEM(y_out, F32), VMEM(block, F32)],
        us=4.0,
    )
    side = (width, HALO, depth)
    rows8 = (width, 8, depth)
    e0, s1, sx, gx, xs1, xs2, ys1, ys2, xf2 = call(
        finish_kernel,
        "step0_planes",
        [(xa1, True), (xa2, True), (rest, True), (sx_own, True), (gx_own, True), (weight, True), (scale, True),
         (modulus, True), (xf2, True), (xs1, True), (xs2, True)],
        [(block, True)] * 4 + [(six, True)] * 2 + [(side, True), (rows8, True), (six, True)],
        aliases={8: 8, 9: 4, 10: 5},
    )
    xs1, xf2, xs2 = swap(xs1, rows1), swap(xf2, rows2), swap(xs2, rows2)
    ys1, ys2 = swap(ys1, cols1), swap(ys2, cols2)
    rest, sx_own, image, fx, fy, image_mod, states = call(
        middle_kernel,
        "images_and_step1_own",
        [(adjoint_in, True), (e0, True), (s1, True), (sx, True), (sy, True), (sz, True), (gy, True), (gz, True),
         (weight, True), (scale, True), (source, True), (forward, True), (xf1, True), (ya1, True),
         (ya2, True), (zf, True), (yf, True)],
        [(block, True)] * 5 + [((1,) + block, False), ((1, STEPS, 1) + block, False)],
        [VMEM(z_out, F32), VMEM(y_out, F32)] + [VMEM(block, F32)] * 4 + [dma((2,))],
        us=20.0,
    )
    rest, image = call(
        column_kernel,
        "column_edges",
        [(ys1, True), (ys2, True), (weight, True), (gy, True), (fy, True), (ye, True), (rest, True), (image, True)],
        [(block, True)] * 2,
        aliases={6: 0, 7: 1},
    )
    image_buo, states = call(
        last_kernel,
        "step1_planes",
        [(xs1, True), (xs2, True), (rest, True), (sx_own, True), (image, True), (fx, True), (gx, True), (weight, True),
         (sx, True), (xf1, True), (xf2, True), (states, False)],
        [((1,) + block, False), ((1, STEPS, 1) + block, False)],
        [VMEM(block, F32), VMEM(block, F32), dma((2 * (height // 8),))],
        aliases={11: 1},
    )
    if lax.axis_size("shot") > 1:
        image_mod, image_buo = lax.psum((image_mod, image_buo), "shot")
    return image_mod, image_buo, states


def solution(mesh):
    placed = (
        P(("grp", "shot"), None, "blk", None, None, None),
        P(("grp", "shot"), None, "blk", None, None, None),
        P(("grp", "blk"), None, None, None),
        P(("grp", "blk"), None, None, None),
        P(("grp", "blk"), None, None),
        P("grp", None),
        P(("grp", "shot"), None, None),
    )
    return jax.shard_map(
        shards,
        mesh=mesh,
        in_specs=placed,
        out_specs=(
            P(("grp", "blk"), None, None, None),
            P(("grp", "blk"), None, None, None),
            P(("grp", "shot"), None, "blk", None, None, None),
        ),
        check_vma=False,
    )
```

```python
import numpy as np
import jax
import jax.numpy as jnp
from jax import lax
from jax.experimental import pallas as pl
from jax.experimental.pallas import tpu as pltpu
from jax.sharding import PartitionSpec as P

STEPS = 2
YBLOCKS = 4
HALO = 4

A0 = -205.0 / 72.0
A = (8.0 / 5.0, -1.0 / 5.0, 8.0 / 315.0, -1.0 / 560.0)
C = (4.0 / 5.0, -1.0 / 5.0, 4.0 / 105.0, -1.0 / 280.0)
A_INT = (8064.0, -1008.0, 128.0, -9.0)
C_INT = (672.0, -168.0, 32.0, -3.0)
A_UNIT = 1.0 / 5040.0
C_UNIT = 1.0 / 840.0
TIME = 0.03
F32 = jnp.float32
BF16 = jnp.bfloat16
VMEM = pltpu.VMEM


def row_pairs(size):
    first, second = [], []
    for i in range(size):
        r = i // YBLOCKS
        partner = i + YBLOCKS if r % 2 == 0 else i - YBLOCKS
        if 0 <= partner < size:
            first.append((i, partner))
        partner = i + YBLOCKS if r % 2 == 1 else i - YBLOCKS
        if 0 <= partner < size:
            second.append((i, partner))
    return first, second


def column_pairs(size):
    first, second = [], []
    for i in range(size):
        c = i % YBLOCKS
        partner = c + 1 if c % 2 == 0 else c - 1
        if 0 <= partner < YBLOCKS:
            first.append((i, i - c + partner))
        partner = c + 1 if c % 2 == 1 else c - 1
        if 0 <= partner < YBLOCKS:
            second.append((i, i - c + partner))
    return first, second


def along_z(depth):
    lap = np.zeros((depth, depth), np.float32)
    slope = np.zeros((depth, depth), np.float32)
    for k in range(1, HALO + 1):
        i = np.arange(depth - k)
        lap[i + k, i] += A_INT[k - 1]
        lap[i, i + k] += A_INT[k - 1]
        slope[i + k, i] += C_INT[k - 1]
        slope[i, i + k] -= C_INT[k - 1]
    return np.concatenate([slope, lap], axis=1)


def along_y(height):
    out = []
    for parity in range(2):
        full = np.zeros((2, height, height + 2 * HALO), np.float32)
        for i in range(height):
            for k in range(1, HALO + 1):
                full[0, i, HALO + i + k] += C_INT[k - 1]
                full[0, i, HALO + i - k] -= C_INT[k - 1]
                full[1, i, HALO + i + k] += A_INT[k - 1]
                full[1, i, HALO + i - k] += A_INT[k - 1]
        full = full.reshape(2 * height, height + 2 * HALO)
        low, own, high = full[:, :HALO], full[:, HALO:-HALO], full[:, -HALO:]
        edge = np.concatenate([high, low] if parity == 0 else [low, high], axis=1)
        out.append(np.concatenate([own, own, edge, edge], axis=1))
    return np.stack(out)


def edge_rows(factor, height):
    rows = np.concatenate([np.arange(8), np.arange(height - 8, height)])
    return factor[:, np.concatenate([rows, height + rows]), 2 * height :]


def parts(value):
    lead = value.astype(BF16)
    return lead, (value - lead.astype(F32)).astype(BF16)


def dot(a, b):
    return jnp.dot(a, b, preferred_element_type=F32)


def z_product(block, factor):
    planes, height, depth = block.shape
    lead, trail = parts(block.reshape(planes * height, depth))
    out = dot(lead, factor) + dot(trail, factor)
    return out.reshape(planes, height, out.shape[1])


def edge_parts(first, second):
    edge = jnp.concatenate([first, second], axis=0)
    lead = edge.astype(BF16).astype(F32)
    return jnp.concatenate([lead, edge - lead], axis=0).astype(BF16)


def y_product(plane, first, second, factor):
    lead, trail = parts(plane)
    return dot(factor, jnp.concatenate([lead, trail, edge_parts(first, second)], axis=0))


def x_slope(own):
    out = []
    for i in range(len(own)):
        total = None
        for k in range(1, HALO + 1):
            if i + k < len(own) and i - k >= 0:
                term = C[k - 1] * (own[i + k] - own[i - k])
            elif i + k < len(own):
                term = C[k - 1] * own[i + k]
            elif i - k >= 0:
                term = -C[k - 1] * own[i - k]
            else:
                continue
            total = term if total is None else total + term
        out.append(total)
    return out


def x_laplace(own):
    out = []
    for i in range(len(own)):
        total = 3.0 * A0 * own[i]
        for k in range(1, HALO + 1):
            if i + k < len(own) and i - k >= 0:
                total = total + A[k - 1] * (own[i + k] + own[i - k])
            elif i + k < len(own):
                total = total + A[k - 1] * own[i + k]
            elif i - k >= 0:
                total = total + A[k - 1] * own[i - k]
        out.append(total)
    return out


def edge_terms(i, count, low, high):
    terms = []
    for k in range(1, HALO + 1):
        if i - k < 0 and low is not None:
            terms.append((k, -1.0, low[HALO + i - k]))
        if i + k >= count and high is not None:
            terms.append((k, 1.0, high[i + k - count]))
    return terms


def edge_slope(i, count, low, high):
    total = None
    for k, sign, value in edge_terms(i, count, low, high):
        term = (sign * C[k - 1]) * value
        total = term if total is None else total + term
    return total


def plus(value, *terms):
    for term in terms:
        value = value if term is None else value + term
    return value


def edge_laplace(i, count, low, high):
    total = None
    for k, _, value in edge_terms(i, count, low, high):
        term = A[k - 1] * value
        total = term if total is None else total + term
    return total


def depth_of_surface(topo_row, height):
    rows = lax.broadcasted_iota(jnp.int32, (height, height), 0)
    lanes = lax.broadcasted_iota(jnp.int32, (height, height), 1)
    picked = jnp.where(rows == lanes, topo_row.astype(F32), 0.0)
    return jnp.sum(picked, axis=1, keepdims=True).astype(jnp.int32)


def four(ref, rows):
    return None if ref is None else [ref[i, rows] for i in range(HALO)]


def two_and_two(first, second, rows):
    return [ref[HALO + i, rows] for ref in (first, second) for i in range(2)]


def row_parity():
    return lax.rem(lax.axis_index("blk") // YBLOCKS, 2)


def column_parity():
    return lax.rem(lax.rem(lax.axis_index("blk"), YBLOCKS), 2)


def copy_all(pairs, sem):
    copies = [pltpu.make_async_copy(a, b, sem.at[n]) for n, (a, b) in enumerate(pairs)]
    for c in copies:
        c.start()
    return copies


def first_kernel(adj, mod, buoy, topo_in, x1, x2, s0, cur_v, mod_v, topo, sem):
    width, height, depth = s0.shape
    parity = row_parity()
    first = pl.ds((1 - parity) * HALO, HALO)
    second = pl.ds(parity * HALO, HALO)
    copies = copy_all(
        [
            (topo_in, topo),
            (adj.at[0, 1, 0], cur_v),
            (mod.at[0], mod_v),
            (buoy.at[0, first], x1.at[0]),
            (buoy.at[0, second], x2.at[0]),
        ],
        sem,
    )
    lanes = lax.broadcasted_iota(jnp.int32, (height, depth), 1)
    copies[0].wait()
    masks = [lanes >= depth_of_surface(topo[0, i : i + 1, :], height) for i in range(width)]
    copies[1].wait()
    copies[2].wait()
    for i in range(width):
        s0[i] = jnp.where(masks[i], mod_v[i] * cur_v[i], 0.0)
    x1[1] = s0[first]
    x2[1] = s0[second]
    for c in copies[3:]:
        c.wait()


def edge_kernel(buoy, fwd, s0, y1, y2, low_v, high_v, sem):
    width, height, depth = s0.shape
    low, high = pl.ds(0, 8), pl.ds(height - 8, 8)
    copies = copy_all(
        [
            (buoy.at[0, :, low], low_v.at[0]),
            (buoy.at[0, :, high], high_v.at[0]),
            (fwd.at[0, pl.ds(1, 2), 0, :, low], low_v.at[pl.ds(1, 2)]),
            (fwd.at[0, pl.ds(1, 2), 0, :, high], high_v.at[pl.ds(1, 2)]),
        ],
        sem,
    )
    even = column_parity() == 0

    def pack(n, low, high):
        y1[n] = jnp.where(even, high, low)
        y2[n] = jnp.where(even, low, high)

    pack(1, s0[:, :HALO], s0[:, height - HALO :])
    for c in copies:
        c.wait()
    for n, m in ((0, 0), (2, 1), (3, 2)):
        pack(n, low_v[m, :, :HALO], high_v[m, :, 8 - HALO :])


def source_kernel(topo, rec, res, fwd, _, scale, source, x1, x2, s1, s2, sem):
    width, height, depth = scale.shape
    parity = row_parity()
    pairs = []
    for out, rest, at in ((x1, s1, (1 - parity) * HALO), (x2, s2, parity * HALO)):
        pairs += [
            (fwd.at[0, 1, 0, pl.ds(at, HALO)], out.at[pl.ds(0, HALO)]),
            (fwd.at[0, 2, 0, pl.ds(at, 2)], out.at[pl.ds(HALO, 2)]),
            (fwd.at[0, 2, 0, pl.ds(at + 2, 2)], rest.at[pl.ds(HALO, 2)]),
        ]
    copies = copy_all(pairs, sem)
    index = lax.axis_index("blk")
    anchor_x = index // YBLOCKS * width
    anchor_y = lax.rem(index, YBLOCKS) * height
    count = rec.shape[1]
    rx = rec[0:1, :] - anchor_x
    ry = rec[1:2, :] - anchor_y
    ids = lax.broadcasted_iota(jnp.int32, (STEPS * width, count), 0)
    values = jnp.concatenate(
        [jnp.broadcast_to(res[0, s : s + 1, :], (width, count)) for s in range(STEPS)], axis=0
    )
    hit_x = jnp.where(lax.rem(ids, width) == rx, values, 0.0)
    hit_y = (lax.broadcasted_iota(jnp.int32, (height, count), 0) == ry).astype(F32)
    plane = lax.dot_general(
        hit_y,
        hit_x,
        (((1,), (1,)), ((), ())),
        precision=lax.Precision.HIGHEST,
        preferred_element_type=F32,
    )
    lanes = lax.broadcasted_iota(jnp.int32, (height, depth), 1)
    for i in range(width):
        surface = depth_of_surface(topo[0, i : i + 1, :], height)
        live = lanes >= surface
        at = lanes == surface + 1
        scale[i] = jnp.where(live, TIME, 0.0)
        for s in range(STEPS):
            n = s * width + i
            source[s, i] = jnp.where(at, plane[:, n : n + 1], 0.0)
    for c in copies:
        c.wait()


def early_kernel(
    adj, buoy, s0, y1, y2, zf, yf, scale, source,
    rest, sx_own, sy, sz, gx_own, gy, gz, weight,
    zs, zb, ys, yb,
):
    width, height, depth = s0.shape
    factor_y = yf[column_parity()]
    zs[...] = z_product(s0[...], zf[...])
    zb[...] = z_product(buoy[0], zf[:, :depth])
    for i in range(width):
        ys[i] = y_product(s0[i], y1[1, i], y2[1, i], factor_y)
        yb[i] = y_product(buoy[0, i], y1[0, i], y2[0, i], factor_y[:height])
    for t in range(height // 8):
        rows = pl.ds(8 * t, 8)
        own = [s0[i, rows] for i in range(width)]
        slope = x_slope(own)
        laplace = x_laplace(own)
        for i in range(width):
            sx_own[i, rows] = slope[i]
            edge = ys[i, pl.ds(height + 8 * t, 8)] + zs[i, rows, depth:]
            laplace[i] = laplace[i] + A_UNIT * edge
        own = [buoy[0, i, rows] for i in range(width)]
        slope = x_slope(own)
        for i in range(width):
            w = scale[i, rows]
            gx_own[i, rows] = slope[i] * w
            g_y = (C_UNIT * w) * yb[i, rows]
            g_z = (C_UNIT * w) * zb[i, rows]
            s_y = C_UNIT * ys[i, rows]
            s_z = C_UNIT * zs[i, rows, :depth]
            b = own[i] * w
            weight[i, rows] = b
            gy[i, rows] = g_y
            gz[i, rows] = g_z
            sy[i, rows] = s_y
            sz[i, rows] = s_z
            moved = 2.0 * adj[0, 1, 0, i, rows] - adj[0, 0, 0, i, rows] + source[0, i, rows]
            moved = jnp.where(w > 0.0, moved, 0.0)
            rest[i, rows] = moved + b * laplace[i] + g_y * s_y + g_z * s_z


def finish_kernel(
    xa1, xa2, rest, sx_own, gx_own, weight, scale, mod, _f2, _x1, _x2,
    e0, s1, sx, gx, x1, x2, y1, y2, f2,
):
    width, height, depth = e0.shape

    def body(low_ref, high_ref, low_out, high_out):
        for t in range(height // 8):
            rows = pl.ds(8 * t, 8)
            low = [low_ref[1, i, rows] for i in range(HALO)]
            high = [high_ref[1, i, rows] for i in range(HALO)]
            low_b = [low_ref[0, i, rows] for i in range(HALO)]
            high_b = [high_ref[0, i, rows] for i in range(HALO)]
            for i in range(width):
                s_x = sx_own[i, rows] + edge_slope(i, width, low, high)
                g_x = gx_own[i, rows] + scale[i, rows] * edge_slope(i, width, low_b, high_b)
                earlier = (
                    rest[i, rows]
                    + weight[i, rows] * edge_laplace(i, width, low, high)
                    + g_x * s_x
                )
                scaled = mod[0, i, rows] * earlier
                sx[i, rows] = s_x
                gx[i, rows] = g_x
                e0[i, rows] = earlier
                s1[i, rows] = scaled
                if i < HALO:
                    low_out[i, rows] = scaled
                if i >= width - HALO:
                    high_out[i - (width - HALO), rows] = scaled

    @pl.when(row_parity() == 0)
    def _():
        body(xa2, xa1, x2, x1)

    @pl.when(row_parity() == 1)
    def _():
        body(xa1, xa2, x1, x2)

    even = column_parity() == 0
    y1[...] = jnp.where(even, s1[:, height - HALO :], s1[:, :HALO])
    y2[...] = jnp.where(even, s1[:, :8], s1[:, height - 8 :])


def middle_kernel(
    adj, e0, s1, sx0, sy0, sz0, gy, gz, weight, scale, source, fwd, xf, yf1, yf2, zf, yf,
    rest, sx_own, image, fx, fy, image_mod, states,
    zs, ys, z1, z2, ya, image_v, sem,
):
    width, height, depth = e0.shape
    first = pltpu.make_async_copy(e0, states.at[0, 0, 0], sem.at[0])
    first.start()
    for i in range(width):
        f0, f1, f2, f3 = (fwd[0, n, 0, i] for n in range(4))
        image_v[i] = adj[0, 1, 0, i] * (f0 - 2.0 * f1 + f2) + e0[i] * (f1 - 2.0 * f2 + f3)
    second = pltpu.make_async_copy(image_v, image_mod.at[0], sem.at[1])
    second.start()
    factor_y = yf[column_parity()]
    factor_own = factor_y[:, : 2 * height]
    zs[...] = z_product(s1[...], zf[...])
    z1[...] = z_product(fwd[0, 1, 0], zf[:, :depth])
    z2[...] = z_product(fwd[0, 2, 0], zf[:, :depth])
    for i in range(width):
        ys[i] = dot(factor_own, jnp.concatenate(parts(s1[i]), axis=0))
        ya[i] = y_product(fwd[0, 1, 0, i], yf1[2, i], yf2[2, i], factor_y[:height])
        fy[i] = y_product(fwd[0, 2, 0, i], yf1[3, i], yf2[3, i], factor_y[:height])

    def body(low_ref, high_ref):
        for t in range(height // 8):
            rows = pl.ds(8 * t, 8)
            own = [s1[i, rows] for i in range(width)]
            slope = x_slope(own)
            laplace = x_laplace(own)
            own1 = [fwd[0, 1, 0, i, rows] for i in range(width)]
            own2 = [fwd[0, 2, 0, i, rows] for i in range(width)]
            slope1 = x_slope(own1)
            slope2 = x_slope(own2)
            low1, high1 = four(low_ref, rows), four(high_ref, rows)
            for i in range(width):
                now, before = adj[0, 1, 0, i, rows], e0[i, rows]
                s_y = C_UNIT * ys[i, rows]
                s_z = C_UNIT * zs[i, rows, :depth]
                edge = ys[i, pl.ds(height + 8 * t, 8)] + zs[i, rows, depth:]
                lap = laplace[i] + A_UNIT * edge
                moved = 2.0 * before - now + source[1, i, rows]
                moved = jnp.where(scale[i, rows] > 0.0, moved, 0.0)
                rest[i, rows] = (
                    moved + weight[i, rows] * lap + gy[i, rows] * s_y + gz[i, rows] * s_z
                )
                sx_own[i, rows] = slope[i]
                f1x = plus(slope1[i], edge_slope(i, width, low1, high1))
                fx[i, rows] = slope2[i]
                image[i, rows] = (
                    f1x * sx0[i, rows]
                    + C_UNIT
                    * (
                        ya[i, rows] * sy0[i, rows]
                        + z1[i, rows] * sz0[i, rows]
                        + fy[i, rows] * s_y
                        + z2[i, rows] * s_z
                    )
                )

    @pl.when(row_parity() == 0)
    def _():
        body(None, xf)

    @pl.when(row_parity() == 1)
    def _():
        body(xf, None)

    first.wait()
    second.wait()


def column_kernel(ys1, ys2, weight, gy, fy, ye, rest_in, image_in, rest, image):
    width, height, depth = weight.shape
    factor = ye[column_parity()]
    even = column_parity() == 0
    for i in range(width):
        second = jnp.where(even, ys2[i, 8 - HALO :], ys2[i, :HALO])
        edge = dot(factor, edge_parts(ys1[i], second))
        for n, start in ((0, 0), (8, height - 8)):
            rows = pl.ds(start, 8)
            s_y = C_UNIT * edge[n : n + 8]
            lap = A_UNIT * edge[16 + n : 24 + n]
            rest[i, rows] = rest_in[i, rows] + weight[i, rows] * lap + gy[i, rows] * s_y
            image[i, rows] = image_in[i, rows] + C_UNIT * (fy[i, rows] * s_y)


def last_kernel(
    xs1, xs2, rest, sx_own, image, fx, gx, weight, sx0, xf1, xf2, states_in,
    image_out, states_out,
    image_v, e1_v, sem,
):
    width, height, depth = rest.shape
    tiles = height // 8

    def leave(t):
        rows = pl.ds(8 * t, 8)
        return (
            pltpu.make_async_copy(e1_v.at[:, rows], states_out.at[0, 1, 0, :, rows], sem.at[t]),
            pltpu.make_async_copy(image_v.at[:, rows], image_out.at[0, :, rows], sem.at[tiles + t]),
        )

    def body(low_ref, high_ref, low_fields, high_fields, low_one, high_one):
        for t in range(tiles):
            rows = pl.ds(8 * t, 8)
            low = [low_ref[i, rows] for i in range(HALO)]
            high = [high_ref[i, rows] for i in range(HALO)]
            low1, high1 = four(low_one, rows), four(high_one, rows)
            low2 = two_and_two(low_fields, low_ref, rows)
            high2 = two_and_two(high_fields, high_ref, rows)
            for i in range(width):
                s_x = sx_own[i, rows] + edge_slope(i, width, low, high)
                lap = edge_laplace(i, width, low, high)
                add = gx[i, rows] * s_x
                f_x = plus(fx[i, rows], edge_slope(i, width, low2, high2))
                shown = image[i, rows] + f_x * s_x
                f_x = edge_slope(i, width, low1, high1)
                if f_x is not None:
                    shown = shown + f_x * sx0[i, rows]
                e1_v[i, rows] = rest[i, rows] + weight[i, rows] * lap + add
                image_v[i, rows] = shown
            for c in leave(t):
                c.start()

    @pl.when(row_parity() == 0)
    def _():
        body(xs2, xs1, xf2, xf1, xf2, None)

    @pl.when(row_parity() == 1)
    def _():
        body(xs1, xs2, xf1, xf2, None, xf2)

    for t in range(tiles):
        for c in leave(t):
            c.wait()


def call(kernel, name, inputs, outputs, scratch=(), us=1.0, aliases=None):
    arrays, in_specs = [], []
    for array, near in inputs:
        place = VMEM if near else pltpu.HBM
        arrays.append(pltpu.with_memory_space_constraint(array, place))
        in_specs.append(pl.BlockSpec(memory_space=place))
    shapes, out_specs = [], []
    for shape, near in outputs:
        place = VMEM if near else pltpu.HBM
        shapes.append(place(shape, F32))
        out_specs.append(pl.BlockSpec(memory_space=place))
    return pl.pallas_call(
        kernel,
        name=name,
        in_specs=in_specs,
        out_specs=out_specs,
        out_shape=shapes,
        scratch_shapes=list(scratch),
        input_output_aliases=aliases or {},
        compiler_params=pltpu.CompilerParams(vmem_limit_bytes=16 * 1024 * 1024),
        cost_estimate=pl.CostEstimate(
            flops=0, bytes_accessed=int(us * 3.0e6), transcendentals=0
        ),
    )(*arrays)


def shards(adjoint_in, forward, modulus, buoyancy, topography, receivers, residuals):
    width, height, depth = modulus.shape[1:]
    block = (width, height, depth)
    size = lax.axis_size("blk")
    rows1, rows2 = row_pairs(size)
    cols1, cols2 = column_pairs(size)
    zf = jnp.asarray(along_z(depth), BF16)
    yf = jnp.asarray(along_y(height), BF16)
    ye = jnp.asarray(edge_rows(along_y(height), height), BF16)
    dma = pltpu.SemaphoreType.DMA

    def swap(value, pairs):
        return lax.ppermute(value, "blk", pairs)

    ahead = (2, HALO, height, depth)
    six = (HALO + 2, height, depth)
    edge = (4, width, HALO, depth)
    xa1, xa2, s0 = call(
        first_kernel,
        "scaled_and_planes",
        [(adjoint_in, False), (modulus, False), (buoyancy, False), (topography, False)],
        [(ahead, True)] * 2 + [(block, True)],
        [VMEM(block, F32), VMEM(block, F32), VMEM(topography.shape, jnp.int32), dma((5,))],
    )
    xa1, xa2 = swap(xa1, rows1), swap(xa2, rows2)
    ya1, ya2 = call(
        edge_kernel,
        "edges",
        [(buoyancy, False), (forward, False), (s0, True)],
        [(edge, True)] * 2,
        [VMEM((3, width, 8, depth), F32), VMEM((3, width, 8, depth), F32), dma((4,))],
    )
    ya1, ya2 = swap(ya1, cols1), swap(ya2, cols2)
    z_out = (width, height, 2 * depth)
    y_out = (width, 2 * height, depth)
    scale, source, xf1, xf2, xs1, xs2 = call(
        source_kernel,
        "sources_and_planes",
        [(topography, True), (receivers.T, True), (residuals, True), (forward, False), (s0, True)],
        [(block, True), ((STEPS,) + block, True)] + [(six, True)] * 4,
        [dma((6,))],
    )
    xf1 = swap(xf1, rows1)
    rest, sx_own, sy, sz, gx_own, gy, gz, weight = call(
        early_kernel,
        "step0_own",
        [(adjoint_in, True), (buoyancy, True), (s0, True), (ya1, True), (ya2, True), (zf, True), (yf, True),
         (scale, True), (source, True)],
        [(block, True)] * 8,
        [VMEM(z_out, F32), VMEM(block, F32), VMEM(y_out, F32), VMEM(block, F32)],
        us=4.0,
    )
    side = (width, HALO, depth)
    rows8 = (width, 8, depth)
    e0, s1, sx, gx, xs1, xs2, ys1, ys2, xf2 = call(
        finish_kernel,
        "step0_planes",
        [(xa1, True), (xa2, True), (rest, True), (sx_own, True), (gx_own, True), (weight, True), (scale, True),
         (modulus, True), (xf2, True), (xs1, True), (xs2, True)],
        [(block, True)] * 4 + [(six, True)] * 2 + [(side, True), (rows8, True), (six, True)],
        aliases={8: 8, 9: 4, 10: 5},
    )
    xs1, xf2, xs2 = swap(xs1, rows1), swap(xf2, rows2), swap(xs2, rows2)
    ys1, ys2 = swap(ys1, cols1), swap(ys2, cols2)
    rest, sx_own, image, fx, fy, image_mod, states = call(
        middle_kernel,
        "images_and_step1_own",
        [(adjoint_in, True), (e0, True), (s1, True), (sx, True), (sy, True), (sz, True), (gy, True), (gz, True),
         (weight, True), (scale, True), (source, True), (forward, True), (xf1, True), (ya1, True),
         (ya2, True), (zf, True), (yf, True)],
        [(block, True)] * 5 + [((1,) + block, False), ((1, STEPS, 1) + block, False)],
        [VMEM(z_out, F32), VMEM(y_out, F32)] + [VMEM(block, F32)] * 4 + [dma((2,))],
        us=20.0,
    )
    rest, image = call(
        column_kernel,
        "column_edges",
        [(ys1, True), (ys2, True), (weight, True), (gy, True), (fy, True), (ye, True), (rest, True), (image, True)],
        [(block, True)] * 2,
        aliases={6: 0, 7: 1},
    )
    image_buo, states = call(
        last_kernel,
        "step1_planes",
        [(xs1, True), (xs2, True), (rest, True), (sx_own, True), (image, True), (fx, True), (gx, True), (weight, True),
         (sx, True), (xf1, True), (xf2, True), (states, False)],
        [((1,) + block, False), ((1, STEPS, 1) + block, False)],
        [VMEM(block, F32), VMEM(block, F32), dma((2 * (height // 8),))],
        aliases={11: 1},
    )
    if lax.axis_size("shot") > 1:
        image_mod, image_buo = lax.psum((image_mod, image_buo), "shot")
    return image_mod, image_buo, states


def solution(mesh):
    placed = (
        P(("grp", "shot"), None, "blk", None, None, None),
        P(("grp", "shot"), None, "blk", None, None, None),
        P(("grp", "blk"), None, None, None),
        P(("grp", "blk"), None, None, None),
        P(("grp", "blk"), None, None),
        P("grp", None),
        P(("grp", "shot"), None, None),
    )
    return jax.shard_map(
        shards,
        mesh=mesh,
        in_specs=placed,
        out_specs=(
            P(("grp", "blk"), None, None, None),
            P(("grp", "blk"), None, None, None),
            P(("grp", "shot"), None, "blk", None, None, None),
        ),
        check_vma=False,
    )
```
